256 devices in a mesh: section: 8 (over z), vocab: 32 (over x, y, core).
Axes of the slice: x: 4, y: 4, z: 8, core: 2. Of those that a mesh axis runs over, the one named last changes fastest.
Arguments:
- section_hidden: bfloat16 [8, 256, 8192], P('section', None, 'vocab'), may hold values from -32 to 32
- norm_gain: float32 [8192], replicated, may hold values from 0.5 to 1.5
- head: bfloat16 [8192, 65536], P(None, ('section', 'vocab')), may hold values from -1 to 1
- teacher_logits: bfloat16 [256, 65536], P(None, ('section', 'vocab')), may hold values from -320 to 320
- exit_layer: int32 [256], replicated, may hold values from 9 to 79, as said below
- row_count: int32 [8], replicated, may hold values from 1 to 64, as said below
- row_index: int32 [8, 64], replicated, may hold values from 0 to 255, as said below
Outputs:
- exit_kl: float32 [8, 64], P('section')
- total_loss: float32 [], replicated
- grad_hidden: bfloat16 [8, 64, 8192], P('section', 'vocab')
The draws below stay inside these ranges and needn't reach their ends.
Inputs may be any that keep to these rules, and one draw needn't show every extreme that they name: `row_index`: every token appears in exactly one used slot over all sections, that of the section of its exit layer; unused slots hold arbitrary token numbers. Some section uses all 64 slots in every draw. `row_count`: the counts add up to 256; some section's count is 64. `exit_layer`: A token scored at section s exits at layer 10 * (s + 1) - 1.
All inputs are finite; a program needn't handle non-finite values.
Results may differ from the reference program's by a relative error of at most 0.0093.
Values may be sent and summed in bfloat16 or wider, within the bound.
A program may use at most 128 MiB of HBM per device.

```python
import math
import jax
import jax.numpy as jnp
from jax import lax

D = 8192
LAYERS = 80
VOCAB = 65536
LAYERS_SECTION = 10
TOKENS = 256
R_MAX = 64
N_SECTION = 8


def plan_exits(key):
    key = jax.random.fold_in(key, 101)
    key_busy, key_weight, key_order, key_filler = jax.random.split(key, 4)
    sections = jnp.arange(N_SECTION, dtype=jnp.int32)
    busiest = jax.random.randint(key_busy, (), 0, N_SECTION, dtype=jnp.int32)
    shares = jax.random.randint(key_weight, (N_SECTION,), 1, 3, dtype=jnp.int32)
    shares = jnp.where(sections == busiest, 0, shares)
    remaining = TOKENS - R_MAX
    counts = shares * remaining // jnp.sum(shares)
    leftover = remaining - jnp.sum(counts)
    ranking = jnp.cumsum((shares > 0).astype(jnp.int32)) - 1
    counts = counts + ((shares > 0) & (ranking < leftover)).astype(jnp.int32)
    counts = jnp.where(sections == busiest, R_MAX, counts).astype(jnp.int32)
    ordering = jax.random.permutation(key_order, TOKENS).astype(jnp.int32)
    endings = jnp.cumsum(counts)
    position = (endings - counts)[:, None] + jnp.arange(R_MAX, dtype=jnp.int32)[None, :]
    filler = jax.random.randint(key_filler, (N_SECTION, R_MAX), 0, TOKENS, dtype=jnp.int32)
    occupied = jnp.arange(R_MAX, dtype=jnp.int32)[None, :] < counts[:, None]
    indices = jnp.where(occupied, ordering[jnp.minimum(position, TOKENS - 1)], filler)
    place_section = jnp.sum((jnp.arange(TOKENS, dtype=jnp.int32)[:, None] >= endings[None, :]).astype(jnp.int32), axis=1)
    token_section = jnp.zeros((TOKENS,), jnp.int32).at[ordering].set(place_section)
    return (token_section, counts, indices.astype(jnp.int32))


def token_kinds(key):
    key = jax.random.fold_in(key, 303)
    return jax.random.randint(key, (TOKENS,), 0, 2, dtype=jnp.int32) == 1


def feature_kinds(key):
    key = jax.random.fold_in(key, 404)
    return jax.random.randint(key, (D,), 0, 2, dtype=jnp.int32) == 1


def draw_exit_layer(key, part):
    token_section, counts, indices = plan_exits(key)
    return ((token_section + 1) * LAYERS_SECTION - 1).astype(jnp.int32)


def draw_row_count(key, part):
    token_section, counts, indices = plan_exits(key)
    return counts


def draw_row_index(key, part):
    token_section, counts, indices = plan_exits(key)
    return indices


def draw_section_hidden(key, part):
    flat_tokens = token_kinds(key)
    strong_features = feature_kinds(key)
    key = jax.random.fold_in(key, 1)
    key_base = jax.random.fold_in(key, 0)
    key_row = jax.random.fold_in(key, 1)
    key_feature = jax.random.fold_in(key, 2)
    key_flat = jax.random.fold_in(key, 5)
    peaked_scale = jnp.exp(jax.random.uniform(key_row, (N_SECTION, TOKENS, 1), jnp.float32, math.log(0.5), math.log(2.0)))
    flat_scale = jnp.exp(jax.random.uniform(key_flat, (N_SECTION, TOKENS, 1), jnp.float32, math.log(0.01), math.log(0.03)))
    row_scale = jnp.where(flat_tokens[None, :, None], flat_scale, peaked_scale)
    feature_scale = jnp.exp(jax.random.uniform(key_feature, (1, 1, D), jnp.float32, -1.15, 1.15))
    kind_factor = jnp.where(flat_tokens[None, :, None] & strong_features[None, None, :], 0.03, 1.0)
    base = jnp.clip(jax.random.normal(key_base, (N_SECTION, TOKENS, D), jnp.float32), -5.0, 5.0)
    values = base * row_scale * feature_scale * kind_factor
    return values.astype(jnp.bfloat16)


def draw_head(key, part):
    strong_features = feature_kinds(key)
    key = jax.random.fold_in(key, 2)
    key_base, key_column = jax.random.split(key)
    column_scale = jnp.exp(jax.random.uniform(key_column, (1, VOCAB), jnp.float32, math.log(0.35), math.log(3.5)))
    feature_factor = jnp.where(strong_features, 4.0, 0.15)[:, None]
    base = jnp.clip(jax.random.normal(key_base, (D, VOCAB), jnp.float32), -5.0, 5.0)
    values = base * (1.0 / math.sqrt(D)) * feature_factor * column_scale
    return values.astype(jnp.bfloat16)


def plant_peaks(values, key):
    key_column, key_height = jax.random.split(key)
    peak_columns = jax.random.randint(key_column, (TOKENS, 8), 0, VOCAB, dtype=jnp.int32)
    heights = jax.random.uniform(key_height, (TOKENS, 8), jnp.float32, 0.5, 3.0)
    row_top = jnp.max(values, axis=1, keepdims=True)
    token_rows = jnp.broadcast_to(jnp.arange(TOKENS, dtype=jnp.int32)[:, None], (TOKENS, 8))
    peaks = jnp.minimum(row_top + heights, 318.0)
    return values.at[token_rows, peak_columns].set(peaks)


def draw_teacher_logits(key, part):
    flat_tokens = token_kinds(key)
    key = jax.random.fold_in(key, 3)
    key_base = jax.random.fold_in(key, 0)
    key_row = jax.random.fold_in(key, 1)
    key_column = jax.random.fold_in(key, 2)
    key_peak = jax.random.fold_in(key, 4)
    key_flat_row = jax.random.fold_in(key, 5)
    key_flat_column = jax.random.fold_in(key, 6)
    row_scale = jnp.exp(jax.random.uniform(key_row, (TOKENS, 1), jnp.float32, math.log(3.0), math.log(12.0)))
    column_scale = 3.0 ** (jnp.arange(VOCAB, dtype=jnp.float32) / VOCAB)[None, :]
    column_scale = column_scale * jnp.exp(jax.random.uniform(key_column, (1, VOCAB), jnp.float32, math.log(0.6), math.log(1.5)))
    flat_row = jnp.exp(jax.random.uniform(key_flat_row, (TOKENS, 1), jnp.float32, math.log(0.15), math.log(0.5)))
    flat_column = jnp.exp(jax.random.uniform(key_flat_column, (1, VOCAB), jnp.float32, math.log(0.7), math.log(1.4)))
    base = jnp.clip(jax.random.normal(key_base, (TOKENS, VOCAB), jnp.float32), -5.0, 5.0)
    peaked = plant_peaks(base * row_scale * column_scale, key_peak)
    flat_values = base * flat_row * flat_column
    values = jnp.where(flat_tokens[:, None], flat_values, peaked)
    return values.astype(jnp.bfloat16)


def setup_inputs(seed: int = 0) -> dict:
    key_list = jax.random.split(jax.random.key(seed), 8)
    section_hidden = draw_section_hidden(jax.random.fold_in(key_list[7], 71), 0)
    norm_gain = jnp.clip(1.0 + 0.1 * jax.random.normal(key_list[1], (D,), jnp.float32), 0.5, 1.5)
    head = draw_head(jax.random.fold_in(key_list[7], 71), 0)
    teacher_logits = draw_teacher_logits(jax.random.fold_in(key_list[7], 71), 0)
    exit_layer = draw_exit_layer(jax.random.fold_in(key_list[7], 71), 0)
    row_count = draw_row_count(jax.random.fold_in(key_list[7], 71), 0)
    row_index = draw_row_index(jax.random.fold_in(key_list[7], 71), 0)
    return dict(section_hidden=section_hidden, norm_gain=norm_gain, head=head, teacher_logits=teacher_logits, exit_layer=exit_layer, row_count=row_count, row_index=row_index)


EPS = 1e-05

def reference(section_hidden, norm_gain, head, teacher_logits, exit_layer, row_count, row_index):
    occupied = jnp.arange(R_MAX, dtype=jnp.int32)[None, :] < row_count[:, None]
    section_grid = jnp.broadcast_to(jnp.arange(N_SECTION, dtype=jnp.int32)[:, None], (N_SECTION, R_MAX))
    target = jnp.where(occupied, row_index, TOKENS).astype(jnp.int32)
    token_section = jnp.zeros((TOKENS,), jnp.int32).at[target.reshape(-1)].set(section_grid.reshape(-1), mode='drop')
    token_ids = jnp.arange(TOKENS, dtype=jnp.int32)
    hidden_rows = section_hidden[token_section, token_ids]
    rows_f32 = hidden_rows.astype(jnp.float32)
    inv_rms = lax.rsqrt(lax.optimization_barrier(jnp.mean(rows_f32 * rows_f32, axis=1, keepdims=True)) + EPS)
    unit_rows = rows_f32 * inv_rms
    gain_f32 = norm_gain.astype(jnp.float32)
    normed = (unit_rows * gain_f32).astype(jnp.bfloat16)
    student = jnp.dot(normed, head, preferred_element_type=jnp.float32)
    teacher = teacher_logits.astype(jnp.float32)
    teacher_lse = jax.nn.logsumexp(teacher, axis=1, keepdims=True)
    student_lse = jax.nn.logsumexp(student, axis=1, keepdims=True)
    target_prob = jnp.exp(teacher - teacher_lse)
    kl_token = lax.optimization_barrier(jnp.sum(target_prob * (teacher - teacher_lse - student + student_lse), axis=1))
    weight = (exit_layer.astype(jnp.float32) + 1.0) / LAYERS
    total_loss = jnp.sum(weight * kl_token) / TOKENS
    dlogit = (weight[:, None] * (jnp.exp(student - student_lse) - target_prob)).astype(jnp.bfloat16)
    grad_normed = lax.dot_general(dlogit, head, (((1,), (1,)), ((), ())), preferred_element_type=jnp.float32)
    scaled = gain_f32 * grad_normed
    grad_token = (inv_rms * (scaled - unit_rows * lax.optimization_barrier(jnp.mean(unit_rows * scaled, axis=1, keepdims=True)))).astype(jnp.bfloat16)
    exit_kl = jnp.where(occupied, kl_token[row_index], jnp.float32(0.0))
    grad_hidden = jnp.where(occupied[:, :, None], grad_token[row_index], jnp.zeros((), jnp.bfloat16))
    return (exit_kl, total_loss, grad_hidden)
```

```python
import functools

import jax
import jax.numpy as jnp
from jax import lax
from jax.experimental import pallas as pl
from jax.experimental.pallas import tpu as pltpu
from jax.sharding import PartitionSpec as P

LAYERS = 80
EPS = 1e-05
F32 = jnp.float32
BF16 = jnp.bfloat16
MESH = pl.DeviceIdType.MESH

NZ, NX, NY, NC = 8, 4, 4, 2
NV = NX * NY * NC
TOK = 256
SLOTS = 64
FC = 256
HALF = TOK // 2
QUART = TOK // 4
OFFS = (0, 1, -1, 2)
PLANE = [(a, b) for a in OFFS for b in OFFS]
PEERS_XY = [o for o in PLANE if o != (0, 0)]
PEERS_Z = (1, -1, 2, -2, 3, -3, 4)
FAR = [(2, 2), (2, 1), (1, 2), (2, -1), (-1, 2), (2, 0), (0, 2), (1, 1), (-1, 1), (1, -1), (-1, -1), (0, 1), (1, 0), (0, -1), (-1, 0), (0, 0)]


class Names:
    def __init__(self):
        self.table = {}

    def __call__(self, *key):
        return self.table.setdefault(key, len(self.table))


def all_names():
    n = Names()
    for d in PEERS_Z:
        n("zrow", d), n("zt", d), n("zs", d), n("zg", d)
    for o in PEERS_XY:
        n("xt", o), n("xs", o), n("tr", o)
    for k in ("ct", "cs", "cr"):
        n(k)
    for p in (0, 1):
        for ph in ("g", "r"):
            for d in OFFS + ("one",):
                for s in (0, 1):
                    n(ph, p, d, "f", s), n(ph, p, d, "h", s)
    for o in PLANE:
        for p in (0, 1):
            n("cg", o, p)
        n("cp", o)
    return n


NAMES = all_names()


def dot(a, b, dims):
    return lax.dot_general(a, b, (dims, ((), ())), preferred_element_type=F32)


def kernel(
    hidden_ref, gain_ref, head_ref, teacher_ref, layer_ref, count_ref, index_ref,
    kl_ref, loss_ref, grad_ref,
    head, rows, zrow, zt, zs, xt, xs, ct, cs,
    hot, cross_out, cross_in, part_sum, half_out, half_in, full_out, full_in,
    z_out, z_in, tr_out, tr_in, tr_side,
    stu, head_sem, send_sem, recv_sem,
):
    z = lax.axis_index("section")
    v = lax.axis_index("vocab")
    x, y, c = v // (NY * NC), lax.rem(v // NC, NY), lax.rem(v, NC)
    other = 1 - c

    def vid(dx, dy, core):
        return (lax.rem(x + dx + NX, NX) * NY + lax.rem(y + dy + NY, NY)) * NC + core

    def qid(dx, dy):
        return lax.rem(x + dx + NX, NX) * NY + lax.rem(y + dy + NY, NY)

    def zid(dz):
        return lax.rem(z + dz + NZ, NZ)

    def to_xy(dx, dy):
        return (z, vid(dx, dy, c))

    def to_z(dz):
        return (zid(dz), v)

    sibling = (z, vid(0, 0, other))
    pending = []

    def copy(name, src, dst, target):
        k = NAMES.table[name]
        return pltpu.make_async_remote_copy(
            src_ref=src, dst_ref=dst, send_sem=send_sem.at[k], recv_sem=recv_sem.at[k],
            device_id=target, device_id_type=MESH)

    def send(name, src, dst, target):
        cp = copy(name, src, dst, target)
        cp.start()
        pending.append(cp)

    def got(name, dst):
        copy(name, dst, dst, sibling).wait_recv()

    barrier = pltpu.get_barrier_semaphore()
    partners = [sibling] + [to_z(d) for d in PEERS_Z] + [to_xy(*o) for o in PEERS_XY]
    for t in partners:
        pl.semaphore_signal(barrier, inc=1, device_id=t, device_id_type=MESH)
    loads = [pltpu.make_async_copy(head_ref.at[pl.ds(8 * i, 8)], head.at[pl.ds(8 * i, 8)], head_sem.at[i]) for i in range(4)]
    for cp in loads:
        cp.start()

    tok_iota = lax.broadcasted_iota(jnp.int32, (TOK, SLOTS), 0)
    slot_iota = lax.broadcasted_iota(jnp.int32, (1, SLOTS), 1)
    own_row = index_ref[pl.ds(z, 1), :]
    pick = (tok_iota == own_row).astype(F32).astype(BF16)
    zrow[z] = dot(pick, hidden_ref[0], ((0,), (0,))).astype(BF16)
    tea = teacher_ref[...].astype(F32).T
    top = jnp.max(tea, axis=0, keepdims=True)
    zt[z, 0:1] = top
    zt[z, 1:2] = jnp.sum(jnp.exp(tea - top), axis=0, keepdims=True)
    pl.semaphore_wait(barrier, len(partners))

    for d in PEERS_Z:
        send(("zrow", d), zrow.at[z], zrow.at[z], to_z(d))
    for d in PEERS_Z:
        send(("zt", d), zt.at[z], zt.at[z], to_z(d))

    for s in range(NZ):
        live_row = jnp.where(slot_iota < count_ref[s], index_ref[s : s + 1, :], -1)
        hot[s] = (tok_iota == live_row).astype(F32).astype(BF16)

    for d in PEERS_Z:
        got(("zrow", d), zrow.at[z])
    mine = dot(hot[0], zrow[0], ((1,), (0,)))
    for s in range(1, NZ):
        mine = mine + dot(hot[s], zrow[s], ((1,), (0,)))
    rows[v] = mine.astype(BF16)
    square = mine * mine
    square = (square[:, :128] + square[:, 128:]).T
    for d in PEERS_Z:
        got(("zt", d), zt.at[z])

    def merge(buf, n, at):
        m = buf[0, at : at + 1]
        for i in range(1, n):
            m = jnp.maximum(m, buf[i, at : at + 1])
        t = jnp.zeros_like(m)
        for i in range(n):
            t = t + buf[i, at + 1 : at + 2] * jnp.exp(buf[i, at : at + 1] - m)
        return m, t

    def total(buf, n, at):
        t = buf[0, at : at + 1]
        for i in range(1, n):
            t = t + buf[i, at : at + 1]
        return t

    q_me = qid(0, 0)
    m, t = merge(zt, NZ, 0)
    xt[q_me, 0:1] = m
    xt[q_me, 1:2] = t
    xt[q_me, 2:3] = jnp.sum(square, axis=0, keepdims=True)
    for o in PEERS_XY:
        send(("xt", o), xt.at[q_me], xt.at[q_me], to_xy(*o))

    def off(p, d1, d2):
        return (d1, d2) if p == 0 else (d2, d1)

    def axis1(p, d):
        return to_xy(d, 0) if p == 0 else to_xy(0, d)

    def axis2(p, d):
        return to_xy(0, d) if p == 0 else to_xy(d, 0)

    def block(p, o, h=None):
        if h is None:
            return rows.at[vid(*o, c), pl.ds(HALF * p, HALF)]
        return rows.at[vid(*o, c), pl.ds(HALF * p + QUART * h, QUART)]

    def relay(p, o):
        send(("cg", o, p), block(p, o), block(p, o), sibling)

    def spread(p, d1):
        o = off(p, d1, 0)
        send(("g", p, d1, "f", 0), block(p, o), block(p, o), axis2(p, 1))
        send(("g", p, d1, "f", 1), block(p, o), block(p, o), axis2(p, -1))

    sides = ((0, -1, 1), (1, 1, -1))
    for p in (0, 1):
        send(("g", p, "one", "f", 0), block(p, (0, 0)), block(p, (0, 0)), axis1(p, 1))
        send(("g", p, "one", "f", 1), block(p, (0, 0)), block(p, (0, 0)), axis1(p, -1))
    for p in (0, 1):
        relay(p, (0, 0))
    for p in (0, 1):
        spread(p, 0)
    for s, frm, to in sides:
        for p in (0, 1):
            o = off(p, frm, 0)
            got(("g", p, "one", "f", s), block(p, o))
            send(("g", p, "one", "h", s), block(p, o, s), block(p, o, s), axis1(p, to))
            spread(p, frm)
            relay(p, o)

    for o in PEERS_XY:
        got(("xt", o), xt.at[q_me])
    m, t = merge(xt, NX * NY, 0)
    ct[c, 0:1] = m
    ct[c, 1:2] = t
    ct[c, 2:3] = total(xt, NX * NY, 2)
    send(("ct",), ct.at[c], ct.at[c], sibling)
    for p in (0, 1):
        o = off(p, 2, 0)
        for s in (0, 1):
            got(("g", p, "one", "h", s), block(p, o, s))
        spread(p, 2)
        relay(p, o)
    got(("ct",), ct.at[c])
    m, t = merge(ct, NC, 0)
    lse_t = m + jnp.log(t)
    inv = lax.rsqrt(total(ct, NC, 2) / (NV * FC) + EPS)
    inv_col = jnp.broadcast_to(inv, (128, TOK)).T
    inv_wide = jnp.concatenate([inv_col, inv_col], axis=1)
    prob = jnp.exp(tea - lse_t)
    for cp in loads:
        cp.wait()

    stu[...] = jnp.zeros_like(stu)

    def score(chunk):
        normed = (rows[chunk].astype(F32) * inv_wide * gain_ref[pl.ds(chunk, 1), :]).astype(BF16)
        stu[...] += dot(normed, head[chunk], ((1,), (0,)))

    score(vid(0, 0, c))
    done = {}

    def arrived(p, o):
        relay(p, o)
        done[o] = done.get(o, 0) + 1
        if done[o] == 2:
            score(vid(*o, c))

    for d1 in (1, -1, 2):
        for p in (0, 1):
            done[off(p, d1, 0)] = done.get(off(p, d1, 0), 0) + 1
    for d1 in OFFS:
        for s, frm, to in sides:
            for p in (0, 1):
                o = off(p, d1, frm)
                got(("g", p, d1, "f", s), block(p, o))
                send(("g", p, d1, "h", s), block(p, o, s), block(p, o, s), axis2(p, to))
                arrived(p, o)
    for d1 in OFFS:
        for p in (0, 1):
            o = off(p, d1, 2)
            for s in (0, 1):
                got(("g", p, d1, "h", s), block(p, o, s))
            arrived(p, o)
    for o in sorted(PLANE, key=lambda o: (2 in o, o != (0, 0))):
        for p in (0, 1):
            got(("cg", o, p), block(p, o))
        score(vid(*o, other))

    student = stu[...].T
    m = jnp.max(student, axis=0, keepdims=True)
    cs[c, 0:1] = m
    cs[c, 1:2] = jnp.sum(jnp.exp(student - m), axis=0, keepdims=True)
    cs[c, 2:3] = jnp.sum(prob * (tea - student), axis=0, keepdims=True)
    send(("cs",), cs.at[c], cs.at[c], sibling)
    got(("cs",), cs.at[c])
    m, t = merge(cs, NC, 0)
    zs[z, 0:1] = m
    zs[z, 1:2] = t
    zs[z, 2:3] = total(cs, NC, 2)
    for d in PEERS_Z:
        send(("zs", d), zs.at[z], zs.at[z], to_z(d))
    for d in PEERS_Z:
        got(("zs", d), zs.at[z])
    m, t = merge(zs, NZ, 0)
    xs[q_me, 0:1] = m
    xs[q_me, 1:2] = t
    xs[q_me, 2:3] = total(zs, NZ, 2)
    for o in PEERS_XY:
        send(("xs", o), xs.at[q_me], xs.at[q_me], to_xy(*o))
    for o in PEERS_XY:
        got(("xs", o), xs.at[q_me])
    m, t = merge(xs, NX * NY, 0)
    lse_s = m + jnp.log(t)
    kl = total(xs, NX * NY, 2) - lse_t + lse_s
    weight = (layer_ref[...].astype(F32) + 1.0) / LAYERS
    dlogit = (weight * (jnp.exp(student - lse_s) - prob)).T.astype(BF16)

    def part(chunk):
        return dot(dlogit, head[chunk], ((1,), (1,)))

    def own(o):
        return PLANE.index(o)

    def give(p, d, ph_axis, h, value):
        half_out[p, d, h] = value.astype(BF16)
        send(("r", p, OFFS[d] if d < 4 else "one", "h", h), half_out.at[p, d, h], half_in.at[p, d, h], ph_axis(p, 1 if h == 0 else -1))

    def settle(o):
        i = own(o)
        got(("cp", o), cross_in.at[i])
        part_sum[i] = part_sum[i] + cross_in[i].astype(F32)
        for p in (0, 1):
            d1, d2 = o if p == 0 else o[::-1]
            if d2 == 2:
                for h in (0, 1):
                    give(p, OFFS.index(d1), axis2, h, part_sum[i, pl.ds(HALF * p + QUART * h, QUART)])

    lag = 3
    for k, o in enumerate(FAR):
        i = own(o)
        cross_out[i] = part(vid(*o, other)).astype(BF16)
        send(("cp", o), cross_out.at[i], cross_in.at[i], sibling)
        part_sum[i] = part(vid(*o, c))
        if k >= lag:
            settle(FAR[k - lag])
    for o in FAR[-lag:]:
        settle(o)

    def pass_on(p, d, axis, near):
        key = OFFS[d] if d < 4 else "one"
        for s in (0, 1):
            got(("r", p, key, "h", s), half_in.at[p, d, s])
            base = QUART * s
            rest = QUART * (1 - s)
            full_out[p, d, s, pl.ds(base, QUART)] = (near(s, base) + half_in[p, d, s].astype(F32)).astype(BF16)
            full_out[p, d, s, pl.ds(rest, QUART)] = near(s, rest).astype(BF16)
            send(("r", p, key, "f", s), full_out.at[p, d, s], full_in.at[p, d, s], axis(p, 1 if s == 0 else -1))

    def collect(p, d):
        key = OFFS[d] if d < 4 else "one"
        for s in (0, 1):
            got(("r", p, key, "f", s), full_in.at[p, d, s])
        return full_in[p, d, 0].astype(F32) + full_in[p, d, 1].astype(F32)

    order = (3, 1, 2, 0)
    for d in order:
        for p in (0, 1):
            def near(s, base, p=p, d=d):
                return part_sum[own(off(p, OFFS[d], 1 if s == 0 else -1)), pl.ds(HALF * p + base, QUART)]
            pass_on(p, d, axis2, near)
    for d in order:
        for p in (0, 1):
            i = own(off(p, OFFS[d], 0))
            part_sum[i, pl.ds(HALF * p, HALF)] = part_sum[i, pl.ds(HALF * p, HALF)] + collect(p, d)
            if d == 3:
                for h in (0, 1):
                    give(p, 4, axis1, h, part_sum[i, pl.ds(HALF * p + QUART * h, QUART)])
    for p in (0, 1):
        def near(s, base, p=p):
            return part_sum[own(off(p, 1 if s == 0 else -1, 0)), pl.ds(HALF * p + base, QUART)]
        pass_on(p, 4, axis1, near)

    hot_own = hot[z]
    two = lax.broadcasted_iota(jnp.int32, (16, SLOTS), 0) + 2 * v == lax.broadcasted_iota(jnp.int32, (16, SLOTS), 1)
    sel_f = dot(two.astype(F32).astype(BF16), hot_own, ((1,), (1,)))
    sel = sel_f.astype(BF16)
    inv_two = jnp.sum(sel_f[0:2] * inv, axis=1, keepdims=True)
    for i in range(NV):
        tr_side[1, i] = dot(sel, rows[i], ((1,), (0,)))[0:2] * inv_two
    kl_col = jnp.broadcast_to(kl, (128, TOK)).T
    kl_ref[...] = jnp.sum(hot_own.astype(F32) * kl_col[:, :SLOTS], axis=0, keepdims=True)
    loss_ref[...] = jnp.sum(weight * kl, axis=1, keepdims=True) / TOK

    i0 = own((0, 0))
    whole = []
    for p in (0, 1):
        whole.append((part_sum[i0, pl.ds(HALF * p, HALF)] + collect(p, 4)).astype(BF16))
    whole = jnp.concatenate(whole, axis=0)

    for d in PEERS_Z:
        k = PEERS_Z.index(d)
        z_out[k] = dot(hot[zid(d)], whole, ((0,), (0,))).astype(BF16)
        send(("zg", d), z_out.at[k], z_in.at[k], to_z(d))
    grads = dot(hot_own, whole, ((0,), (0,)))
    for d in PEERS_Z:
        k = PEERS_Z.index(d)
        got(("zg", d), z_in.at[k])
        grads = grads + z_in[k].astype(F32)
    for q in range(NX * NY):
        for cc in range(NC):
            j = (q * NC + cc) * 2
            tr_out[q, cc] = grads[j : j + 2]
    for o in PEERS_XY:
        send(("tr", o), tr_out.at[qid(*o)], tr_in.at[q_me], to_xy(*o))
    tr_in[q_me] = tr_out[q_me]
    for o in PEERS_XY:
        got(("tr", o), tr_in.at[q_me])
    send(("cr",), tr_in.at[:, other], tr_side.at[0, pl.ds(0, 16)], sibling)
    got(("cr",), tr_side.at[0, pl.ds(0, 16)])
    both = []
    acc = jnp.zeros((2, FC), F32)
    for q in range(NX * NY):
        for cc in range(NC):
            i = q * NC + cc
            dn = jnp.where(c == cc, tr_in[q, cc], tr_side[0, q]) * gain_ref[i : i + 1, :]
            both.append(dn)
            acc = acc + dn * tr_side[1, i]
    mean = jnp.sum(acc, axis=1, keepdims=True) / (NV * FC)
    for i in range(NV):
        grad_ref[0, :, FC * i : FC * (i + 1)] = (inv_two * (both[i] - tr_side[1, i] * mean)).astype(BF16)
    for cp in pending:
        cp.wait_send()


def on_device(section_hidden, norm_gain, head, teacher_logits, exit_layer, row_count, row_index):
    vmem = pl.BlockSpec(memory_space=pltpu.VMEM)
    n = len(NAMES.table)
    exit_kl, loss, grad = pl.pallas_call(
        kernel,
        out_shape=(
            jax.ShapeDtypeStruct((1, SLOTS), F32),
            jax.ShapeDtypeStruct((1, 1), F32),
            jax.ShapeDtypeStruct((1, 2, NV * FC), BF16),
        ),
        in_specs=[vmem, vmem, pl.BlockSpec(memory_space=pl.ANY), vmem, vmem, pl.BlockSpec(memory_space=pltpu.SMEM), vmem],
        out_specs=(vmem, vmem, vmem),
        scratch_shapes=[
            pltpu.VMEM((NV, FC, TOK), BF16),
            pltpu.VMEM((NV, TOK, FC), BF16),
            pltpu.VMEM((NZ, SLOTS, FC), BF16),
            pltpu.VMEM((NZ, 4, TOK), F32),
            pltpu.VMEM((NZ, 4, TOK), F32),
            pltpu.VMEM((NX * NY, 4, TOK), F32),
            pltpu.VMEM((NX * NY, 4, TOK), F32),
            pltpu.VMEM((NC, 4, TOK), F32),
            pltpu.VMEM((NC, 4, TOK), F32),
            pltpu.VMEM((NZ, TOK, SLOTS), BF16),
            pltpu.VMEM((16, TOK, FC), BF16),
            pltpu.VMEM((16, TOK, FC), BF16),
            pltpu.VMEM((16, TOK, FC), F32),
            pltpu.VMEM((2, 5, 2, QUART, FC), BF16),
            pltpu.VMEM((2, 5, 2, QUART, FC), BF16),
            pltpu.VMEM((2, 5, 2, HALF, FC), BF16),
            pltpu.VMEM((2, 5, 2, HALF, FC), BF16),
            pltpu.VMEM((7, SLOTS, FC), BF16),
            pltpu.VMEM((7, SLOTS, FC), BF16),
            pltpu.VMEM((16, 2, 2, FC), F32),
            pltpu.VMEM((16, 2, 2, FC), F32),
            pltpu.VMEM((2, NV, 2, FC), F32),
            pltpu.VMEM((TOK, 256), F32),
            pltpu.SemaphoreType.DMA((4,)),
            pltpu.SemaphoreType.DMA((n,)),
            pltpu.SemaphoreType.DMA((n,)),
        ],
        compiler_params=pltpu.CompilerParams(collective_id=0, has_side_effects=True, vmem_limit_bytes=48 * 2**20),
        name="exit_loss",
    )(
        section_hidden,
        norm_gain.reshape(NV, FC),
        head.reshape(NV, FC, head.shape[1]),
        teacher_logits,
        exit_layer.reshape(1, TOK),
        row_count,
        row_index,
    )
    return exit_kl, loss.reshape(()), grad


def solution(mesh):
    return jax.shard_map(
        on_device,
        mesh=mesh,
        in_specs=(
            P("section", None, "vocab"),
            P(),
            P(None, ("section", "vocab")),
            P(None, ("section", "vocab")),
            P(),
            P(),
            P(),
        ),
        out_specs=(P("section", None), P(), P("section", "vocab", None)),
        check_vma=False,
    )
```

```python
import jax
import jax.numpy as jnp
from jax import lax
from jax.experimental import pallas as pl
from jax.experimental.pallas import tpu as pltpu
from jax.sharding import PartitionSpec as P

LAYERS = 80
EPS = 1e-05
F32 = jnp.float32
BF16 = jnp.bfloat16
MESH = pl.DeviceIdType.MESH

NZ, NX, NY, NC = 8, 4, 4, 2
NV = NX * NY * NC
TOK = 256
SLOTS = 64
FC = 256
HF = FC // 2
HT = TOK // 2
OFFS = (0, 1, -1, 2)
PLANE = [(a, b) for a in OFFS for b in OFFS]
PEERS_XY = sorted((o for o in PLANE if o != (0, 0)), key=lambda o: -abs(o[0]) - abs(o[1]))
PEERS_Z = (4, 3, -3, 2, -2, 1, -1)
FAR = [(2, 2), (2, 1), (1, 2), (2, -1), (-1, 2), (2, 0), (0, 2), (1, 1), (-1, 1), (1, -1), (-1, -1), (0, 1), (1, 0), (0, -1), (-1, 0), (0, 0)]


RING_G = (0, 1, -1)
RING_R = (0, 1, -1)


def all_names():
    names = ["z0", "z1", "zt", "xt", "ct", "cs", "zs", "xs", "zg0", "zg1", "tr", "cr"]
    names += [("ring", p, d, k) for p in (0, 1) for d in OFFS + ("one",) for k in range(3)]
    names += [("core", o) for o in PLANE]
    return {k: i for i, k in enumerate(names)}


NAMES = all_names()
GROUPS = {k: i for i, k in enumerate(["z0", "z1", "zt", "xt", "ct", "cs", "zs", "xs", "zg0", "zg1", "tr", "cr", "g", "r", "cg", "cr2"])}


def dot(a, b, dims):
    return lax.dot_general(a, b, (dims, ((), ())), preferred_element_type=F32)


def kernel(
    hidden_hbm, gain_hbm, head_hbm, teacher_hbm, layer_hbm, count_hbm, index_hbm,
    out_ref,
    hidden_ref, gain_ref, teacher_ref, layer_ref, count_ref, index_ref, head,
    rows, zrow, zt, zs, xt, xs, ct, cs,
    hot, cross_out, cross_in, part_sum, half_out, half_in, full_out, full_in,
    z_out, z_in, tr_out, tr_in, tr_side, unit_ref,
    stu, load_sem, head_sem, send_sem, recv_sem,
):
    z = lax.axis_index("section")
    v = lax.axis_index("vocab")
    x, y, c = v // (NY * NC), lax.rem(v // NC, NY), lax.rem(v, NC)
    other = 1 - c

    def qid(dx, dy):
        return lax.rem(x + dx + NX, NX) * NY + lax.rem(y + dy + NY, NY)

    def vid(dx, dy, core):
        return qid(dx, dy) * NC + core

    def zid(dz):
        return lax.rem(z + dz + NZ, NZ)

    def to_xy(dx, dy):
        return (z, vid(dx, dy, c))

    def to_z(dz):
        return (zid(dz), v)

    sibling = (z, vid(0, 0, other))

    def send(group, name, src, dst, target):
        pltpu.make_async_remote_copy(
            src_ref=src, dst_ref=dst, send_sem=send_sem.at[GROUPS[group]], recv_sem=recv_sem.at[NAMES[name]],
            device_id=target, device_id_type=MESH).start()

    def got(name, dst):
        pltpu.make_async_copy(dst, dst, recv_sem.at[NAMES[name]]).wait()

    def sent(group, src):
        pltpu.make_async_copy(src, src, send_sem.at[GROUPS[group]]).wait()

    def gain(chunk):
        return jnp.concatenate([gain_ref[pl.ds(2 * chunk, 1), :], gain_ref[pl.ds(2 * chunk + 1, 1), :]], axis=1)

    barrier = pltpu.get_barrier_semaphore()
    partners = [to_z(d) for d in PEERS_Z] + [to_xy(*o) for o in PEERS_XY] + [sibling]
    for t in partners:
        pl.semaphore_signal(barrier, inc=1, device_id=t, device_id_type=MESH)
    small = [(index_hbm, index_ref), (hidden_hbm, hidden_ref), (teacher_hbm, teacher_ref), (count_hbm, count_ref), (gain_hbm, gain_ref), (layer_hbm, layer_ref)]
    small = [pltpu.make_async_copy(a, b, load_sem.at[i]) for i, (a, b) in enumerate(small)]
    loads = [pltpu.make_async_copy(head_hbm.at[pl.ds(8 * i, 8)], head.at[pl.ds(8 * i, 8)], head_sem.at[i]) for i in range(4)]
    for cp in small + loads:
        cp.start()
    for cp in small:
        cp.wait()

    tok_iota = lax.broadcasted_iota(jnp.int32, (TOK, SLOTS), 0)
    slot_iota = lax.broadcasted_iota(jnp.int32, (1, SLOTS), 1)
    own_row = index_ref[pl.ds(z, 1), :]
    pick = (tok_iota == own_row).astype(F32).astype(BF16)
    picked = dot(pick, hidden_ref[0], ((0,), (0,))).astype(BF16)
    for p in (0, 1):
        zrow[p, z] = picked[:, HF * p : HF * (p + 1)]
    tea = teacher_ref[...].astype(F32).T
    top = jnp.max(tea, axis=0, keepdims=True)
    zt[z, 0:1] = top
    zt[z, 1:2] = jnp.sum(jnp.exp(tea - top), axis=0, keepdims=True)
    for s in range(NZ):
        live_row = jnp.where(slot_iota < count_ref[s], index_ref[s : s + 1, :], -1)
        hot[s] = (tok_iota == live_row).astype(F32).astype(BF16)
    pl.semaphore_wait(barrier, len(partners))
    for p in (0, 1):
        for d in PEERS_Z:
            send("z%d" % p, "z%d" % p, zrow.at[p, z], zrow.at[p, z], to_z(d))
    for d in PEERS_Z:
        send("zt", "zt", zt.at[z], zt.at[z], to_z(d))

    def off(p, d1, d2):
        return (d1, d2) if p == 0 else (d2, d1)

    def axis1(p, d):
        return to_xy(d, 0) if p == 0 else to_xy(0, d)

    def axis2(p, d):
        return to_xy(0, d) if p == 0 else to_xy(d, 0)

    def block(p, o, h=None, core=None):
        at = vid(*o, c if core is None else core)
        if h is None:
            return rows.at[at, p]
        return rows.at[at, p, pl.ds(HT * h, HT)]

    def relay(p, o):
        send("cg", ("core", o), block(p, o), block(p, o), sibling)

    sides = ((0, -1, 1), (1, 1, -1))

    def spread(p, d, o, axis):
        if d not in RING_G:
            send("g", ("ring", p, d, 2), block(p, o), block(p, o), axis(p, 2))
        send("g", ("ring", p, d, 0), block(p, o), block(p, o), axis(p, 1))
        send("g", ("ring", p, d, 1), block(p, o), block(p, o), axis(p, -1))

    def forward(p, d, o, s, axis):
        if d in RING_G:
            send("g", ("ring", p, d, 2), block(p, o, s), block(p, o, s), axis(p, sides[s][2]))

    squares = None
    for p in (0, 1):
        got("z%d" % p, zrow.at[p, pl.ds(0, NZ - 1)])
        mine = dot(hot[0], zrow[p, 0], ((1,), (0,)))
        for s in range(1, NZ):
            mine = mine + dot(hot[s], zrow[p, s], ((1,), (0,)))
        rows[v, p] = mine.astype(BF16)
        spread(p, "one", (0, 0), axis1)
        spread(p, 0, (0, 0), axis2)
        relay(p, (0, 0))
        squares = mine * mine if p == 0 else squares + mine * mine
    squares = squares.T

    def merge(buf, n, at):
        m = buf[0, at : at + 1]
        for i in range(1, n):
            m = jnp.maximum(m, buf[i, at : at + 1])
        t = jnp.zeros_like(m)
        for i in range(n):
            t = t + buf[i, at + 1 : at + 2] * jnp.exp(buf[i, at : at + 1] - m)
        return m, t

    def total(buf, n, at):
        t = buf[0, at : at + 1]
        for i in range(1, n):
            t = t + buf[i, at : at + 1]
        return t

    got("zt", zt.at[pl.ds(0, NZ - 1)])
    q_me = qid(0, 0)
    m, t = merge(zt, NZ, 0)
    xt[q_me, 0:1] = m
    xt[q_me, 1:2] = t
    xt[q_me, 2:3] = jnp.sum(squares, axis=0, keepdims=True)
    for o in PEERS_XY:
        send("xt", "xt", xt.at[q_me], xt.at[q_me], to_xy(*o))

    have = {(0, 0): 2}
    ready = []

    def arrived(p, o):
        relay(p, o)
        have[o] = have.get(o, 0) + 1
        if have[o] == 2:
            ready.append((o, c))

    for p in (0, 1):
        for s, frm, to in sides:
            o = off(p, frm, 0)
            got(("ring", p, "one", s), block(p, o))
            forward(p, "one", o, s, axis1)
            spread(p, frm, o, axis2)
            arrived(p, o)

    got("xt", xt.at[pl.ds(0, NX * NY - 1)])
    m, t = merge(xt, NX * NY, 0)
    ct[c, 0:1] = m
    ct[c, 1:2] = t
    ct[c, 2:3] = total(xt, NX * NY, 2)
    send("ct", "ct", ct.at[c], ct.at[c], sibling)
    for p in (0, 1):
        o = off(p, 2, 0)
        got(("ring", p, "one", 2), block(p, o))
        spread(p, 2, o, axis2)
        arrived(p, o)

    stu[...] = jnp.zeros_like(stu)
    for cp in loads:
        cp.wait()
    got("ct", ct.at[c])
    m, t = merge(ct, NC, 0)
    lse_t = m + jnp.log(t)
    inv = lax.rsqrt(total(ct, NC, 2) / (NV * FC) + EPS)
    inv_col = jnp.broadcast_to(inv, (HF, TOK)).T
    inv_wide = jnp.concatenate([inv_col, inv_col], axis=1)

    def score(chunk):
        raw = jnp.concatenate([rows[chunk, 0], rows[chunk, 1]], axis=1)
        normed = (raw.astype(F32) * inv_wide * gain(chunk)).astype(BF16)
        stu[...] += dot(normed, head[chunk], ((1,), (0,)))

    def score_sibling(o):
        got(("core", o), rows.at[vid(*o, other)])
        score(vid(*o, other))

    scored = []

    def drain(lag):
        while ready:
            o, _ = ready.pop(0)
            score(vid(*o, c))
            scored.append(o)
        while len(scored) > lag:
            score_sibling(scored.pop(0))

    ready.insert(0, ((0, 0), c))
    for d in (0, 1, -1):
        for p in (0, 1):
            for s, frm, to in sides:
                o = off(p, d, frm)
                got(("ring", p, d, s), block(p, o))
                forward(p, d, o, s, axis2)
                arrived(p, o)
        drain(4)
    prob = jnp.exp(tea - lse_t)
    weight = (layer_ref[...].astype(F32) + 1.0) / LAYERS
    for d in (0, 2, 1, -1):
        for p in (0, 1):
            if d == 2:
                for s, frm, to in sides:
                    o = off(p, d, frm)
                    got(("ring", p, d, s), block(p, o))
                    forward(p, d, o, s, axis2)
                    arrived(p, o)
            o = off(p, d, 2)
            got(("ring", p, d, 2), block(p, o))
            arrived(p, o)
        drain(3)
    drain(0)
    student = stu[...].T
    m = jnp.max(student, axis=0, keepdims=True)
    cs[c, 0:1] = m
    cs[c, 1:2] = jnp.sum(jnp.exp(student - m), axis=0, keepdims=True)
    cs[c, 2:3] = jnp.sum(prob * (tea - student), axis=0, keepdims=True)
    send("cs", "cs", cs.at[c], cs.at[c], sibling)
    got("cs", cs.at[c])
    m, t = merge(cs, NC, 0)
    zs[z, 0:1] = m
    zs[z, 1:2] = t
    zs[z, 2:3] = total(cs, NC, 2)
    for d in PEERS_Z:
        send("zs", "zs", zs.at[z], zs.at[z], to_z(d))
    got("zs", zs.at[pl.ds(0, NZ - 1)])
    m, t = merge(zs, NZ, 0)
    xs[q_me, 0:1] = m
    xs[q_me, 1:2] = t
    xs[q_me, 2:3] = total(zs, NZ, 2)
    for o in PEERS_XY:
        send("xs", "xs", xs.at[q_me], xs.at[q_me], to_xy(*o))
    got("xs", xs.at[pl.ds(0, NX * NY - 1)])
    m, t = merge(xs, NX * NY, 0)
    lse_s = m + jnp.log(t)
    kl = total(xs, NX * NY, 2) - lse_t + lse_s
    dlogit = (weight * (jnp.exp(student - lse_s) - prob)).T.astype(BF16)
    def part(chunk):
        return dot(dlogit, head[chunk], ((1,), (1,)))

    def own(o):
        return PLANE.index(o)

    def slot(d):
        return OFFS.index(d) if d != "one" else 4

    def chunk_at(p, d, d1):
        return own(off(p, d1, 0)) if d == "one" else own(off(p, d, d1))

    def give(p, d, d1, axis):
        i, k = chunk_at(p, d, d1), slot(d)
        if d not in RING_R:
            j = (1, -1, 2).index(d1)
            full_out[p, k, j] = part_sum[i, p].astype(BF16)
            send("r", ("ring", p, d, 2), full_out.at[p, k, j], full_in.at[p, k, j], axis(p, d1))
        elif d1 == 2:
            for h in (0, 1):
                half_out[p, k, h] = part_sum[i, p, pl.ds(HT * h, HT)].astype(BF16)
                send("r", ("ring", p, d, h), half_out.at[p, k, h], half_in.at[p, k, h], axis(p, 1 - 2 * h))

    def pass_on(p, d, axis):
        if d not in RING_R:
            return
        k = slot(d)
        for s in (0, 1):
            i = chunk_at(p, d, 1 - 2 * s)
            got(("ring", p, d, s), half_in.at[p, k, s])
            near = pl.ds(HT * s, HT)
            rest = pl.ds(HT * (1 - s), HT)
            full_out[p, k, s, near] = (part_sum[i, p, near] + half_in[p, k, s].astype(F32)).astype(BF16)
            full_out[p, k, s, rest] = part_sum[i, p, rest].astype(BF16)
            send("r", ("ring", p, d, 2), full_out.at[p, k, s], full_in.at[p, k, s], axis(p, 1 - 2 * s))

    def collect(p, d):
        i, k = chunk_at(p, d, 0), slot(d)
        n = 2 if d in RING_R else 3
        got(("ring", p, d, 2), full_in.at[p, k, pl.ds(0, n)])
        value = part_sum[i, p]
        for j in range(n):
            value = value + full_in[p, k, j].astype(F32)
        return value

    def settle(o):
        i = own(o)
        got(("core", o), cross_in.at[i])
        for p in (0, 1):
            part_sum[i, p] = part_sum[i, p] + cross_in[i, p].astype(F32)
            d1, d2 = o[::-1] if p == 0 else o
            if d1 != 0:
                give(p, d2, d1, axis2)

    lag = 3
    for k, o in enumerate(FAR):
        i = own(o)
        value = part(vid(*o, other)).astype(BF16)
        for p in (0, 1):
            cross_out[i, p] = value[:, HF * p : HF * (p + 1)]
        send("cr2", ("core", o), cross_out.at[i], cross_in.at[i], sibling)
        value = part(vid(*o, c))
        for p in (0, 1):
            part_sum[i, p] = value[:, HF * p : HF * (p + 1)]
        if k >= lag:
            settle(FAR[k - lag])
    for o in FAR[-lag:]:
        settle(o)

    for p in (0, 1):
        pass_on(p, 2, axis2)
    for p in (0, 1):
        pass_on(p, 1, axis2)
        pass_on(p, -1, axis2)
    for d in (2, 1, -1):
        for p in (0, 1):
            part_sum[chunk_at(p, d, 0), p] = collect(p, d)
            give(p, "one", d, axis1)
        if d == 2:
            for p in (0, 1):
                pass_on(p, 0, axis2)
    for p in (0, 1):
        pass_on(p, "one", axis1)
    for p in (0, 1):
        part_sum[own((0, 0)), p] = collect(p, 0)

    hot_own = hot[z]
    two = lax.broadcasted_iota(jnp.int32, (16, SLOTS), 0) + 2 * v == lax.broadcasted_iota(jnp.int32, (16, SLOTS), 1)
    sel_f = dot(two.astype(F32).astype(BF16), hot_own, ((1,), (1,)))
    sel = sel_f.astype(BF16)
    inv_two = jnp.sum(sel_f[0:2] * inv, axis=1, keepdims=True)
    for i in range(NV):
        for p in (0, 1):
            unit_ref[:, pl.ds(FC * i + HF * p, HF)] = dot(sel, rows[i, p], ((1,), (0,)))[0:2] * inv_two
    kl_col = jnp.broadcast_to(kl, (HF, TOK)).T
    out_ref[0:1, NV * FC : NV * FC + SLOTS] = jnp.sum(hot_own.astype(F32) * kl_col[:, :SLOTS], axis=0, keepdims=True)
    out_ref[1:2, NV * FC : NV * FC + 1] = jnp.sum(weight * kl, axis=1, keepdims=True) / TOK

    mine = []
    for p in (0, 1):
        whole = collect(p, "one").astype(BF16)
        for k, d in enumerate(PEERS_Z):
            z_out[p, k] = dot(hot[zid(d)], whole, ((0,), (0,))).astype(BF16)
            send("zg%d" % p, "zg%d" % p, z_out.at[p, k], z_in.at[p, k], to_z(d))
        mine.append(dot(hot_own, whole, ((0,), (0,))))
    grads = []
    for p in (0, 1):
        got("zg%d" % p, z_in.at[p])
        value = mine[p]
        for k in range(NZ - 1):
            value = value + z_in[p, k].astype(F32)
        grads.append(value)
    grads = jnp.concatenate(grads, axis=1)
    for q in range(NX * NY):
        for cc in range(NC):
            j = (q * NC + cc) * 2
            tr_out[q, cc] = grads[j : j + 2]
    for k, o in enumerate(PEERS_XY):
        send("tr", "tr", tr_out.at[qid(*o)], tr_in.at[q_me], to_xy(*o))
    tr_in[q_me] = tr_out[q_me]
    got("tr", tr_in.at[pl.ds(0, NX * NY - 1)])
    send("cr", "cr", tr_in.at[:, other], tr_side, sibling)
    got("cr", tr_side)
    both = []
    acc = jnp.zeros((2, FC), F32)
    for q in range(NX * NY):
        for cc in range(NC):
            i = q * NC + cc
            dn = jnp.where(c == cc, tr_in[q, cc], tr_side[q]) * gain(i)
            both.append(dn)
            acc = acc + dn * unit_ref[:, FC * i : FC * (i + 1)]
    mean = jnp.sum(acc, axis=1, keepdims=True) / (NV * FC)
    for i in range(NV):
        at = slice(FC * i, FC * (i + 1))
        out_ref[:, at] = inv_two * (both[i] - unit_ref[:, at] * mean)
    for k in ("z0", "z1"):
        sent(k, zrow.at[0, pl.ds(0, NZ - 1)])
    for k in ("zt", "zs"):
        sent(k, zt.at[pl.ds(0, NZ - 1)])
    for k in ("xt", "xs"):
        sent(k, xt.at[pl.ds(0, NX * NY - 1)])
    for k in ("ct", "cs"):
        sent(k, ct.at[c])
    for k in ("g", "r"):
        sent(k, rows.at[pl.ds(0, 15)])
    for k in ("cg", "cr2"):
        sent(k, rows.at[pl.ds(0, 16)])
    for k in ("zg0", "zg1"):
        sent(k, z_out.at[0])
    sent("tr", tr_out.at[pl.ds(0, NX * NY - 1)])
    sent("cr", tr_side)


def on_device(section_hidden, norm_gain, head, teacher_logits, exit_layer, row_count, row_index):
    packed = pl.pallas_call(
        kernel,
        out_shape=pltpu.VMEM((2, NV * FC + 128), F32),
        in_specs=[pl.BlockSpec(memory_space=pltpu.HBM)] * 7,
        out_specs=pl.BlockSpec(memory_space=pltpu.VMEM),
        scratch_shapes=[
            pltpu.VMEM((1, TOK, FC), BF16),
            pltpu.VMEM((2 * NV, 128), F32),
            pltpu.VMEM((TOK, FC), BF16),
            pltpu.VMEM((1, TOK), jnp.int32),
            pltpu.SMEM((NZ,), jnp.int32),
            pltpu.VMEM((NZ, SLOTS), jnp.int32),
            pltpu.VMEM((NV, FC, TOK), BF16),
            pltpu.VMEM((NV, 2, TOK, HF), BF16),
            pltpu.VMEM((2, NZ, SLOTS, HF), BF16),
            pltpu.VMEM((NZ, 4, TOK), F32),
            pltpu.VMEM((NZ, 4, TOK), F32),
            pltpu.VMEM((NX * NY, 4, TOK), F32),
            pltpu.VMEM((NX * NY, 4, TOK), F32),
            pltpu.VMEM((NC, 4, TOK), F32),
            pltpu.VMEM((NC, 4, TOK), F32),
            pltpu.VMEM((NZ, TOK, SLOTS), BF16),
            pltpu.VMEM((16, 2, TOK, HF), BF16),
            pltpu.VMEM((16, 2, TOK, HF), BF16),
            pltpu.VMEM((16, 2, TOK, HF), F32),
            pltpu.VMEM((2, 5, 2, HT, HF), BF16),
            pltpu.VMEM((2, 5, 2, HT, HF), BF16),
            pltpu.VMEM((2, 5, 3, TOK, HF), BF16),
            pltpu.VMEM((2, 5, 3, TOK, HF), BF16),
            pltpu.VMEM((2, NZ - 1, SLOTS, HF), BF16),
            pltpu.VMEM((2, NZ - 1, SLOTS, HF), BF16),
            pltpu.VMEM((16, 2, 2, FC), F32),
            pltpu.VMEM((16, 2, 2, FC), F32),
            pltpu.VMEM((16, 2, FC), F32),
            pltpu.VMEM((2, NV * FC), F32),
            pltpu.VMEM((TOK, 256), F32),
            pltpu.SemaphoreType.DMA((6,)),
            pltpu.SemaphoreType.DMA((4,)),
            pltpu.SemaphoreType.DMA((len(GROUPS),)),
            pltpu.SemaphoreType.DMA((len(NAMES),)),
        ],
        compiler_params=pltpu.CompilerParams(collective_id=0, has_side_effects=True, vmem_limit_bytes=60 * 2**20),
        name="exit_loss",
    )(
        section_hidden,
        norm_gain.reshape(2 * NV, 128),
        head.reshape(NV, FC, head.shape[1]),
        teacher_logits,
        exit_layer.reshape(1, TOK),
        row_count,
        row_index,
    )
    wide = NV * FC
    return packed[0:1, wide : wide + SLOTS], packed[1, wide], packed[None, :, :wide].astype(BF16)


def solution(mesh):
    return jax.shard_map(
        on_device,
        mesh=mesh,
        in_specs=(
            P("section", None, "vocab"),
            P(),
            P(None, ("section", "vocab")),
            P(None, ("section", "vocab")),
            P(),
            P(),
            P(),
        ),
        out_specs=(P("section", None), P(), P("section", "vocab", None)),
        check_vma=False,
    )
```

```python
import jax
import jax.numpy as jnp
from jax import lax
from jax.experimental import pallas as pl
from jax.experimental.pallas import tpu as pltpu
from jax.sharding import PartitionSpec as P

LAYERS = 80
EPS = 1e-05
F32 = jnp.float32
BF16 = jnp.bfloat16
MESH = pl.DeviceIdType.MESH

NZ, NX, NY, NC = 8, 4, 4, 2
NV = NX * NY * NC
TOK = 256
SLOTS = 64
FC = 256
HF = FC // 2
HT = TOK // 2
OFFS = (0, 1, -1, 2)
PLANE = [(a, b) for a in OFFS for b in OFFS]
PEERS_XY = sorted((o for o in PLANE if o != (0, 0)), key=lambda o: -abs(o[0]) - abs(o[1]))
PEERS_Z = (4, 3, -3, 2, -2, 1, -1)
NP = NZ * NC
FAR = [(2, 2), (2, 1), (1, 2), (2, -1), (-1, 2), (2, 0), (0, 2), (1, 1), (-1, 1), (1, -1), (-1, -1), (0, 1), (1, 0), (0, -1), (-1, 0), (0, 0)]


RING_G = (0, 1, -1)
RING_R = (0,)


def all_names():
    names = ["z0", "z1", "zt", "xt", "zs", "xs", "zg0", "zg1", "tr"]
    names += [("ring", p, d, k) for p in (0, 1) for d in OFFS + ("one",) for k in range(3)]
    names += [("core", o) for o in PLANE]
    return {k: i for i, k in enumerate(names)}


NAMES = all_names()
GROUPS = {k: i for i, k in enumerate(["z0", "z1", "zt", "xt", "zs", "xs", "zg0", "zg1", "tr", "g", "r", "cg", "cr2"])}


def dot(a, b, dims):
    return lax.dot_general(a, b, (dims, ((), ())), preferred_element_type=F32)


def kernel(
    hidden_hbm, gain_hbm, head_hbm, teacher_hbm, layer_hbm, count_hbm, index_hbm,
    out_ref,
    hidden_ref, gain_ref, teacher_ref, layer_ref, count_ref, index_ref, head,
    rows, zrow, zt, zs, xt, xs,
    hot, hot_all, hot_t, cross_out, cross_in, part_sum, half_out, half_in, full_out, full_in,
    z_out, z_in, tr_out, tr_in, unit_ref,
    stu, load_sem, head_sem, send_sem, recv_sem,
):
    z = lax.axis_index("section")
    v = lax.axis_index("vocab")
    x, y, c = v // (NY * NC), lax.rem(v // NC, NY), lax.rem(v, NC)
    other = 1 - c

    def qid(dx, dy):
        return lax.rem(x + dx + NX, NX) * NY + lax.rem(y + dy + NY, NY)

    def vid(dx, dy, core):
        return qid(dx, dy) * NC + core

    def zid(dz):
        return lax.rem(z + dz + NZ, NZ)

    def to_xy(dx, dy):
        return (z, vid(dx, dy, c))

    def to_z(dz):
        return (zid(dz), v)

    def column(dz, core):
        return (zid(dz), vid(0, 0, core))

    sibling = (z, vid(0, 0, other))
    pairs = [(d, k) for d in PEERS_Z for k in (0, 1)] + [(0, 1)]
    me = z * NC + c

    def to_pair(d, k):
        return column(d, c if k == 0 else other)

    def send(group, name, src, dst, target):
        pltpu.make_async_remote_copy(
            src_ref=src, dst_ref=dst, send_sem=send_sem.at[GROUPS[group]], recv_sem=recv_sem.at[NAMES[name]],
            device_id=target, device_id_type=MESH).start()

    def got(name, dst):
        pltpu.make_async_copy(dst, dst, recv_sem.at[NAMES[name]]).wait()

    def sent(group, src):
        pltpu.make_async_copy(src, src, send_sem.at[GROUPS[group]]).wait()

    def gain(chunk):
        return jnp.concatenate([gain_ref[pl.ds(2 * chunk, 1), :], gain_ref[pl.ds(2 * chunk + 1, 1), :]], axis=1)

    barrier = pltpu.get_barrier_semaphore()
    partners = [to_pair(*o) for o in pairs] + [to_xy(*o) for o in PEERS_XY]
    for t in partners:
        pl.semaphore_signal(barrier, inc=1, device_id=t, device_id_type=MESH)
    small = [(index_hbm, index_ref), (hidden_hbm, hidden_ref), (teacher_hbm, teacher_ref), (count_hbm, count_ref), (gain_hbm, gain_ref), (layer_hbm, layer_ref)]
    small = [pltpu.make_async_copy(a, b, load_sem.at[i]) for i, (a, b) in enumerate(small)]
    loads = [pltpu.make_async_copy(head_hbm.at[pl.ds(8 * i, 8)], head.at[pl.ds(8 * i, 8)], head_sem.at[i]) for i in range(4)]
    for cp in small + loads:
        cp.start()
    for cp in small:
        cp.wait()

    tok_iota = lax.broadcasted_iota(jnp.int32, (TOK, SLOTS), 0)
    slot_iota = lax.broadcasted_iota(jnp.int32, (1, SLOTS), 1)
    own_row = index_ref[pl.ds(z, 1), :]
    pick = (tok_iota == own_row).astype(F32).astype(BF16)
    picked = dot(pick, hidden_ref[0], ((0,), (0,))).astype(BF16)
    for p in (0, 1):
        zrow[p, z] = picked[:, HF * p : HF * (p + 1)]
    squares = picked.astype(F32)
    squares = squares * squares
    squares = (squares[:, :HF] + squares[:, HF:]).T
    q_me = qid(0, 0)
    tea = teacher_ref[...].astype(F32).T
    top = jnp.max(tea, axis=0, keepdims=True)
    xt[q_me, 0:1] = top
    xt[q_me, 1:2] = jnp.sum(jnp.exp(tea - top), axis=0, keepdims=True)
    xt[q_me, 2:3, 0:SLOTS] = jnp.sum(squares, axis=0, keepdims=True)
    for s in range(NZ):
        live_row = jnp.where(slot_iota < count_ref[s], index_ref[s : s + 1, :], -1)
        hot[s] = (tok_iota == live_row).astype(F32).astype(BF16)
        hot_all[:, SLOTS * s : SLOTS * (s + 1)] = hot[s]
    pl.semaphore_wait(barrier, len(partners))
    for d in PEERS_Z:
        send("z0", "z0", zrow.at[0, z], zrow.at[0, z], to_z(d))
    for o in PEERS_XY:
        send("xt", "xt", xt.at[q_me], xt.at[q_me], to_xy(*o))
    for d in PEERS_Z:
        send("z1", "z1", zrow.at[1, z], zrow.at[1, z], to_z(d))

    row = lax.broadcasted_iota(jnp.int32, (SLOTS, SLOTS), 0)
    col = lax.broadcasted_iota(jnp.int32, (SLOTS, SLOTS), 1)
    perm = (row == 4 * ((col % 32) // 2) + 2 * (col // 32) + col % 2).astype(F32).astype(BF16)
    for s in range(NZ):
        hot_t[s] = dot(hot[s], perm, ((1,), (0,))).T.astype(BF16)

    def off(p, d1, d2):
        return (d1, d2) if p == 0 else (d2, d1)

    def axis1(p, d):
        return to_xy(d, 0) if p == 0 else to_xy(0, d)

    def axis2(p, d):
        return to_xy(0, d) if p == 0 else to_xy(d, 0)

    def block(p, o, h=None, core=None):
        at = vid(*o, c if core is None else core)
        if h is None:
            return rows.at[at, p]
        return rows.at[at, p, pl.ds(HT * h, HT)]

    def relay(p, o):
        send("cg", ("core", o), block(p, o), block(p, o), sibling)

    sides = ((0, -1, 1), (1, 1, -1))

    def spread(p, d, o, axis):
        send("g", ("ring", p, d, 0), block(p, o), block(p, o), axis(p, 1))
        send("g", ("ring", p, d, 1), block(p, o), block(p, o), axis(p, -1))
        if d not in RING_G:
            send("g", ("ring", p, d, 2), block(p, o), block(p, o), axis(p, 2))

    def forward(p, d, o, s, axis):
        if d in RING_G:
            send("g", ("ring", p, d, 2), block(p, o, s), block(p, o, s), axis(p, sides[s][2]))

    def merge(buf, n, at):
        m = buf[0, at : at + 1]
        for i in range(1, n):
            m = jnp.maximum(m, buf[i, at : at + 1])
        t = jnp.zeros_like(m)
        for i in range(n):
            t = t + buf[i, at + 1 : at + 2] * jnp.exp(buf[i, at : at + 1] - m)
        return m, t

    def total(buf, n, at):
        t = buf[0, at : at + 1]
        for i in range(1, n):
            t = t + buf[i, at : at + 1]
        return t

    have = {(0, 0): 2}
    ready = []

    def arrived(p, o):
        relay(p, o)
        have[o] = have.get(o, 0) + 1
        if have[o] == 2:
            ready.append((o, c))

    def start(p):
        got("z%d" % p, zrow.at[p, pl.ds(0, NZ - 1)])
        mine = dot(hot_all[...], zrow[p].reshape(NZ * SLOTS, HF), ((1,), (0,)))
        rows[v, p] = mine.astype(BF16)
        spread(p, "one", (0, 0), axis1)
        spread(p, 0, (0, 0), axis2)
        relay(p, (0, 0))

    def first(p):
        for s, frm, to in sides:
            o = off(p, frm, 0)
            got(("ring", p, "one", s), block(p, o))
            forward(p, "one", o, s, axis1)
            spread(p, frm, o, axis2)
            arrived(p, o)
        for s, frm, to in sides:
            o = off(p, 0, frm)
            got(("ring", p, 0, s), block(p, o))
            forward(p, 0, o, s, axis2)
            arrived(p, o)
        o = off(p, 2, 0)
        got(("ring", p, "one", 2), block(p, o))
        spread(p, 2, o, axis2)
        arrived(p, o)

    start(0)
    got("xt", xt.at[pl.ds(0, NX * NY - 1)])
    m, t = merge(xt, NX * NY, 0)
    zt[me, 0:1] = m
    zt[me, 1:2] = t
    zt[me, 2:3] = total(xt, NX * NY, 2)
    for o in pairs:
        send("zt", "zt", zt.at[me], zt.at[me], to_pair(*o))
    start(1)
    first(0)
    first(1)
    stu[...] = jnp.zeros_like(stu)
    for cp in loads:
        cp.wait()
    got("zt", zt.at[pl.ds(0, NP - 1)])
    m, t = merge(zt, NP, 0)
    lse_t = m + jnp.log(t)
    spots = jnp.zeros((TOK, SLOTS), F32)

    def inverse(s):
        return lax.rsqrt((zt[NC * s, 2:3, 0:SLOTS] + zt[NC * s + 1, 2:3, 0:SLOTS]) / (NV * FC) + EPS)

    for s in range(NZ):
        spots = spots + hot[s].astype(F32) * inverse(s)
    inv_wide = jnp.broadcast_to(jnp.sum(spots, axis=1, keepdims=True), (TOK, FC))

    def score(chunk):
        raw = jnp.concatenate([rows[chunk, 0], rows[chunk, 1]], axis=1)
        normed = (raw.astype(F32) * inv_wide * gain(chunk)).astype(BF16)
        stu[...] += dot(normed, head[chunk], ((1,), (0,)))

    def score_sibling(o):
        got(("core", o), rows.at[vid(*o, other)])
        score(vid(*o, other))

    scored = []

    def drain(lag):
        while ready:
            o, _ = ready.pop(0)
            score(vid(*o, c))
            scored.append(o)
        while len(scored) > lag:
            score_sibling(scored.pop(0))

    ready.insert(0, ((0, 0), c))
    drain(4)
    for d in (1, -1):
        for p in (0, 1):
            for s, frm, to in sides:
                o = off(p, d, frm)
                got(("ring", p, d, s), block(p, o))
                forward(p, d, o, s, axis2)
                arrived(p, o)
        drain(4)
    prob = jnp.exp(tea - lse_t)
    weight = (layer_ref[...].astype(F32) + 1.0) / LAYERS
    for d in (0, 2, 1, -1):
        for p in (0, 1):
            if d == 2:
                for s, frm, to in sides:
                    o = off(p, d, frm)
                    got(("ring", p, d, s), block(p, o))
                    forward(p, d, o, s, axis2)
                    arrived(p, o)
            o = off(p, d, 2)
            got(("ring", p, d, 2), block(p, o))
            arrived(p, o)
        drain(3)
    drain(0)
    student = stu[...].T
    m = jnp.max(student, axis=0, keepdims=True)
    zs[me, 0:1] = m
    zs[me, 1:2] = jnp.sum(jnp.exp(student - m), axis=0, keepdims=True)
    zs[me, 2:3] = jnp.sum(prob * (tea - student), axis=0, keepdims=True)
    for o in pairs:
        send("zs", "zs", zs.at[me], zs.at[me], to_pair(*o))
    got("zs", zs.at[pl.ds(0, NP - 1)])
    m, t = merge(zs, NP, 0)
    xs[q_me, 0:1] = m
    xs[q_me, 1:2] = t
    xs[q_me, 2:3] = total(zs, NP, 2)
    for o in PEERS_XY:
        send("xs", "xs", xs.at[q_me], xs.at[q_me], to_xy(*o))
    got("xs", xs.at[pl.ds(0, NX * NY - 1)])
    m, t = merge(xs, NX * NY, 0)
    lse_s = m + jnp.log(t)
    kl = total(xs, NX * NY, 2) - lse_t + lse_s
    dlogit = (weight * (jnp.exp(student - lse_s) - prob)).T.astype(BF16)
    def part(chunk):
        return dot(dlogit, head[chunk], ((1,), (1,)))

    def own(o):
        return PLANE.index(o)

    def slot(d):
        return OFFS.index(d) if d != "one" else 4

    def chunk_at(p, d, d1):
        return own(off(p, d1, 0)) if d == "one" else own(off(p, d, d1))

    def give(p, d, d1, axis, value):
        i, k = chunk_at(p, d, d1), slot(d)
        if d1 != 0 and d not in RING_R:
            j = (1, -1, 2).index(d1)
            full_out[p, k, j] = value.astype(BF16)
            send("r", ("ring", p, d, 2), full_out.at[p, k, j], full_in.at[p, k, j], axis(p, d1))
        elif d1 == 2:
            for h in (0, 1):
                half_out[p, k, h] = value[HT * h : HT * (h + 1)].astype(BF16)
                send("r", ("ring", p, d, h), half_out.at[p, k, h], half_in.at[p, k, h], axis(p, 1 - 2 * h))
        else:
            part_sum[i, p] = value

    def pass_on(p, d, axis):
        if d not in RING_R:
            return
        k = slot(d)
        for s in (0, 1):
            i = chunk_at(p, d, 1 - 2 * s)
            got(("ring", p, d, s), half_in.at[p, k, s])
            near = pl.ds(HT * s, HT)
            rest = pl.ds(HT * (1 - s), HT)
            full_out[p, k, s, near] = (part_sum[i, p, near] + half_in[p, k, s].astype(F32)).astype(BF16)
            full_out[p, k, s, rest] = part_sum[i, p, rest].astype(BF16)
            send("r", ("ring", p, d, 2), full_out.at[p, k, s], full_in.at[p, k, s], axis(p, 1 - 2 * s))

    def collect(p, d):
        i, k = chunk_at(p, d, 0), slot(d)
        n = 2 if d in RING_R else 3
        got(("ring", p, d, 2), full_in.at[p, k, pl.ds(0, n)])
        value = part_sum[i, p]
        for j in range(n):
            value = value + full_in[p, k, j].astype(F32)
        return value

    def settle(o):
        i = own(o)
        value = part(vid(*o, c))
        got(("core", o), cross_in.at[i])
        for p in (0, 1):
            d1, d2 = o[::-1] if p == 0 else o
            give(p, d2, d1, axis2, value[:, HF * p : HF * (p + 1)] + cross_in[i, p].astype(F32))

    lag = 3
    for k, o in enumerate(FAR):
        value = part(vid(*o, other)).astype(BF16)
        for p in (0, 1):
            cross_out[own(o), p] = value[:, HF * p : HF * (p + 1)]
        send("cr2", ("core", o), cross_out.at[own(o)], cross_in.at[own(o)], sibling)
        if k >= lag:
            settle(FAR[k - lag])
    for o in FAR[-lag:]:
        settle(o)

    for d in (2, 1, -1):
        for p in (0, 1):
            pass_on(p, d, axis2)
        for p in (0, 1):
            if d == 2:
                give(p, "one", d, axis1, collect(p, d))
    for p in (0, 1):
        pass_on(p, 0, axis2)
    for d in (1, -1):
        for p in (0, 1):
            give(p, "one", d, axis1, collect(p, d))
    for p in (0, 1):
        pass_on(p, "one", axis1)
    for p in (0, 1):
        part_sum[own((0, 0)), p] = collect(p, 0)

    hot_own = hot[z]
    two = lax.broadcasted_iota(jnp.int32, (16, SLOTS), 0) + 2 * v == lax.broadcasted_iota(jnp.int32, (16, SLOTS), 1)
    sel_f = dot(two.astype(F32).astype(BF16), hot_own, ((1,), (1,)))
    sel = sel_f.astype(BF16)
    own_inv = inverse(z) * jnp.where(slot_iota < count_ref[z], 1.0, 0.0)
    inv_two = jnp.sum(two[0:2].astype(F32) * own_inv, axis=1, keepdims=True)
    for i in range(NV):
        for p in (0, 1):
            unit_ref[:, pl.ds(FC * i + HF * p, HF)] = dot(sel, rows[i, p], ((1,), (0,)))[0:2] * inv_two
    kl_col = jnp.broadcast_to(kl, (HF, TOK)).T
    out_ref[0:1, NV * FC : NV * FC + SLOTS] = jnp.sum(hot_own.astype(F32) * kl_col[:, :SLOTS], axis=0, keepdims=True)
    out_ref[1:2, NV * FC : NV * FC + 1] = jnp.sum(weight * kl, axis=1, keepdims=True) / TOK

    for p in (0, 1):
        whole = collect(p, "one").astype(BF16)
        spread_rows = dot(hot_t[...].reshape(NZ * SLOTS, TOK), whole, ((1,), (0,))).astype(BF16)
        for s in range(NZ):
            for k in range(NC):
                at = SLOTS * s + 32 * k
                z_out[p, NC * s + k] = spread_rows[at : at + 32]
        for d, k in pairs:
            to = NC * zid(d) + (c if k == 0 else other)
            send("zg%d" % p, "zg%d" % p, z_out.at[p, to], z_in.at[p, me], to_pair(d, k))
        z_in[p, me] = z_out[p, me]
    grads = []
    for p in (0, 1):
        got("zg%d" % p, z_in.at[p, pl.ds(0, NP - 1)])
        for k in range(NC):
            value = z_in[p, k].astype(F32)
            for s in range(1, NZ):
                value = value + z_in[p, NC * s + k].astype(F32)
            grads.append(value)
    grads = jnp.concatenate([grads[0], grads[2], grads[1], grads[3]], axis=1)
    for q in range(NX * NY):
        tr_out[q] = grads[2 * q : 2 * q + 2]
    for o in PEERS_XY:
        send("tr", "tr", tr_out.at[qid(*o)], tr_in.at[q_me], to_xy(*o))
    tr_in[q_me] = tr_out[q_me]
    got("tr", tr_in.at[pl.ds(0, NX * NY - 1)])
    both = []
    acc = jnp.zeros((2, FC), F32)
    for i in range(NV):
        dn = tr_in[i // 2, :, FC * (i % 2) : FC * (i % 2 + 1)] * gain(i)
        both.append(dn)
        acc = acc + dn * unit_ref[:, FC * i : FC * (i + 1)]
    mean = jnp.sum(acc, axis=1, keepdims=True) / (NV * FC)
    for i in range(NV):
        at = slice(FC * i, FC * (i + 1))
        out_ref[:, at] = inv_two * (both[i] - unit_ref[:, at] * mean)
    for k in ("z0", "z1"):
        sent(k, zrow.at[0, pl.ds(0, NZ - 1)])
    for k in ("zt", "zs"):
        sent(k, zt.at[pl.ds(0, NP - 1)])
    for k in ("xt", "xs"):
        sent(k, xt.at[pl.ds(0, NX * NY - 1)])
    for k in ("g", "r"):
        sent(k, rows.at[pl.ds(0, 15)])
    for k in ("cg", "cr2"):
        sent(k, rows.at[pl.ds(0, 16)])
    for k in ("zg0", "zg1"):
        sent(k, z_out.at[0, pl.ds(0, NP - 1)])
    sent("tr", tr_out.at[pl.ds(0, NX * NY - 1)])


def on_device(section_hidden, norm_gain, head, teacher_logits, exit_layer, row_count, row_index):
    packed = pl.pallas_call(
        kernel,
        out_shape=pltpu.VMEM((2, NV * FC + 128), F32),
        in_specs=[pl.BlockSpec(memory_space=pltpu.HBM)] * 7,
        out_specs=pl.BlockSpec(memory_space=pltpu.VMEM),
        scratch_shapes=[
            pltpu.VMEM((1, TOK, FC), BF16),
            pltpu.VMEM((2 * NV, 128), F32),
            pltpu.VMEM((TOK, FC), BF16),
            pltpu.VMEM((1, TOK), jnp.int32),
            pltpu.SMEM((NZ,), jnp.int32),
            pltpu.VMEM((NZ, SLOTS), jnp.int32),
            pltpu.VMEM((NV, FC, TOK), BF16),
            pltpu.VMEM((NV, 2, TOK, HF), BF16),
            pltpu.VMEM((2, NZ, SLOTS, HF), BF16),
            pltpu.VMEM((NP, 4, TOK), F32),
            pltpu.VMEM((NP, 4, TOK), F32),
            pltpu.VMEM((NX * NY, 4, TOK), F32),
            pltpu.VMEM((NX * NY, 4, TOK), F32),
            pltpu.VMEM((NZ, TOK, SLOTS), BF16),
            pltpu.VMEM((TOK, NZ * SLOTS), BF16),
            pltpu.VMEM((NZ, SLOTS, TOK), BF16),
            pltpu.VMEM((16, 2, TOK, HF), BF16),
            pltpu.VMEM((16, 2, TOK, HF), BF16),
            pltpu.VMEM((16, 2, TOK, HF), F32),
            pltpu.VMEM((2, 5, 2, HT, HF), BF16),
            pltpu.VMEM((2, 5, 2, HT, HF), BF16),
            pltpu.VMEM((2, 5, 3, TOK, HF), BF16),
            pltpu.VMEM((2, 5, 3, TOK, HF), BF16),
            pltpu.VMEM((2, NP, 32, HF), BF16),
            pltpu.VMEM((2, NP, 32, HF), BF16),
            pltpu.VMEM((NX * NY, 2, NC * FC), F32),
            pltpu.VMEM((NX * NY, 2, NC * FC), F32),
            pltpu.VMEM((2, NV * FC), F32),
            pltpu.VMEM((TOK, 256), F32),
            pltpu.SemaphoreType.DMA((6,)),
            pltpu.SemaphoreType.DMA((4,)),
            pltpu.SemaphoreType.DMA((len(GROUPS),)),
            pltpu.SemaphoreType.DMA((len(NAMES),)),
        ],
        compiler_params=pltpu.CompilerParams(collective_id=0, has_side_effects=True, vmem_limit_bytes=60 * 2**20),
        name="exit_loss",
    )(
        section_hidden,
        norm_gain.reshape(2 * NV, 128),
        head.reshape(NV, FC, head.shape[1]),
        teacher_logits,
        exit_layer.reshape(1, TOK),
        row_count,
        row_index,
    )
    wide = NV * FC
    return packed[0:1, wide : wide + SLOTS], packed[1, wide], packed[None, :, :wide].astype(BF16)


def solution(mesh):
    return jax.shard_map(
        on_device,
        mesh=mesh,
        in_specs=(
            P("section", None, "vocab"),
            P(),
            P(None, ("section", "vocab")),
            P(None, ("section", "vocab")),
            P(),
            P(),
            P(),
        ),
        out_specs=(P("section", None), P(), P("section", "vocab", None)),
        check_vma=False,
    )
```

```python
import jax
import jax.numpy as jnp
from jax import lax
from jax.experimental import pallas as pl
from jax.experimental.pallas import tpu as pltpu
from jax.sharding import PartitionSpec as P

LAYERS = 80
EPS = 1e-05
F32 = jnp.float32
BF16 = jnp.bfloat16
MESH = pl.DeviceIdType.MESH

NZ, NX, NY, NC = 8, 4, 4, 2
NV = NX * NY * NC
TOK = 256
SLOTS = 64
FC = 256
HF = FC // 2
HT = TOK // 2
OFFS = (0, 1, -1, 2)
PLANE = [(a, b) for a in OFFS for b in OFFS]
PEERS_XY = sorted((o for o in PLANE if o != (0, 0)), key=lambda o: -abs(o[0]) - abs(o[1]))
PEERS_Z = (4, 3, -3, 2, -2, 1, -1)
NP = NZ * NC
FAR = [(2, 2), (2, 1), (1, 2), (2, -1), (-1, 2), (2, 0), (0, 2), (1, 1), (-1, 1), (1, -1), (-1, -1), (0, 1), (1, 0), (0, -1), (-1, 0), (0, 0)]


RING_G = ((0,), (0,))
RING_R = ((0,), (0,))


def all_names():
    names = ["z0", "z1", "zt", "xt", "zs", "xs", "zg0", "zg1", "tr", "hd", "st", "tc", "un"]
    names += [("ring", p, d, k) for p in (0, 1) for d in OFFS + ("one",) for k in range(3)]
    return {k: i for i, k in enumerate(names)}


NAMES = all_names()
GROUPS = {k: i for i, k in enumerate(["z0", "z1", "zt", "xt", "zs", "xs", "zg0", "zg1", "tr", "g", "r", "hd", "st", "tc", "un"])}


def dot(a, b, dims):
    return lax.dot_general(a, b, (dims, ((), ())), preferred_element_type=F32)


def kernel(
    hidden_hbm, gain_hbm, head_hbm, teacher_hbm, layer_hbm, count_hbm, index_hbm,
    out_ref,
    hidden_ref, gain_ref, teacher_ref, layer_ref, count_ref, index_ref, head,
    rows, zrow, zt, zs, xt, xs,
    hot, hot_all, hot_t, teacher_sib, part_sum, half_out, half_in, full_out, full_in,
    z_out, z_in, tr_out, tr_in, unit_own, unit_out, unit_sib,
    stu, stu_in, load_sem, head_sem, send_sem, recv_sem,
):
    z = lax.axis_index("section")
    v = lax.axis_index("vocab")
    x, y, c = v // (NY * NC), lax.rem(v // NC, NY), lax.rem(v, NC)
    other = 1 - c

    def qid(dx, dy):
        return lax.rem(x + dx + NX, NX) * NY + lax.rem(y + dy + NY, NY)

    def vid(dx, dy, core):
        return qid(dx, dy) * NC + core

    def zid(dz):
        return lax.rem(z + dz + NZ, NZ)

    def to_xy(dx, dy):
        return (z, vid(dx, dy, c))

    def to_z(dz):
        return (zid(dz), v)

    def column(dz, core):
        return (zid(dz), vid(0, 0, core))

    sibling = (z, vid(0, 0, other))
    pairs = [(d, k) for d in PEERS_Z for k in (0, 1)] + [(0, 1)]
    me = z * NC + c

    def to_pair(d, k):
        return column(d, c if k == 0 else other)

    def send(group, name, src, dst, target):
        pltpu.make_async_remote_copy(
            src_ref=src, dst_ref=dst, send_sem=send_sem.at[GROUPS[group]], recv_sem=recv_sem.at[NAMES[name]],
            device_id=target, device_id_type=MESH).start()

    def got(name, dst):
        pltpu.make_async_copy(dst, dst, recv_sem.at[NAMES[name]]).wait()

    def sent(group, src):
        pltpu.make_async_copy(src, src, send_sem.at[GROUPS[group]]).wait()

    def gain(chunk):
        return jnp.concatenate([gain_ref[pl.ds(2 * chunk, 1), :], gain_ref[pl.ds(2 * chunk + 1, 1), :]], axis=1)

    barrier = pltpu.get_barrier_semaphore()
    partners = [to_pair(*o) for o in pairs] + [to_xy(*o) for o in PEERS_XY]
    for t in partners:
        pl.semaphore_signal(barrier, inc=1, device_id=t, device_id_type=MESH)
    small = [(index_hbm, index_ref), (hidden_hbm, hidden_ref), (teacher_hbm, teacher_ref), (count_hbm, count_ref), (gain_hbm, gain_ref), (layer_hbm, layer_ref)]
    small = [pltpu.make_async_copy(a, b, load_sem.at[i]) for i, (a, b) in enumerate(small)]
    loads = [pltpu.make_async_copy(head_hbm.at[pl.ds(4 * i, 4), c], head.at[pl.ds(4 * i, 4), :, pl.ds(0, FC)], head_sem.at[i]) for i in range(4)]
    for cp in small + loads:
        cp.start()
    for cp in small:
        cp.wait()

    tok_iota = lax.broadcasted_iota(jnp.int32, (TOK, SLOTS), 0)
    slot_iota = lax.broadcasted_iota(jnp.int32, (1, SLOTS), 1)
    own_row = index_ref[pl.ds(z, 1), :]
    pick = (tok_iota == own_row).astype(F32).astype(BF16)
    picked = dot(pick, hidden_ref[0], ((0,), (0,))).astype(BF16)
    for p in (0, 1):
        zrow[p, z] = picked[:, HF * p : HF * (p + 1)]
    squares = picked.astype(F32)
    squares = squares * squares
    squares = (squares[:, :HF] + squares[:, HF:]).T
    q_me = qid(0, 0)
    tea = teacher_ref[...].astype(F32).T
    top = jnp.max(tea, axis=0, keepdims=True)
    xt[q_me, 0:1] = top + jnp.log(jnp.sum(jnp.exp(tea - top), axis=0, keepdims=True))
    xt[q_me, 1:2, 0:SLOTS] = jnp.sum(squares, axis=0, keepdims=True)
    for s in range(NZ):
        live_row = jnp.where(slot_iota < count_ref[s], index_ref[s : s + 1, :], -1)
        hot[s] = (tok_iota == live_row).astype(F32).astype(BF16)
        hot_all[:, SLOTS * s : SLOTS * (s + 1)] = hot[s]
    pl.semaphore_wait(barrier, len(partners))
    for d in PEERS_Z:
        send("z0", "z0", zrow.at[0, z], zrow.at[0, z], to_z(d))
    for o in PEERS_XY:
        send("xt", "xt", xt.at[q_me], xt.at[q_me], to_xy(*o))
    for d in PEERS_Z:
        send("z1", "z1", zrow.at[1, z], zrow.at[1, z], to_z(d))

    head_side = head.at[:, :, pl.ds(FC, FC)]
    send("tc", "tc", teacher_ref, teacher_sib, sibling)
    send("hd", "hd", head_hbm.at[:, other], head_side, sibling)

    row = lax.broadcasted_iota(jnp.int32, (SLOTS, SLOTS), 0)
    col = lax.broadcasted_iota(jnp.int32, (SLOTS, SLOTS), 1)
    perm = (row == 4 * ((col % 32) // 2) + 2 * (col // 32) + col % 2).astype(F32).astype(BF16)
    for s in range(NZ):
        hot_t[s] = dot(hot[s], perm, ((1,), (0,))).T.astype(BF16)

    def off(p, d1, d2):
        return (d1, d2) if p == 0 else (d2, d1)

    def axis1(p, d):
        return to_xy(d, 0) if p == 0 else to_xy(0, d)

    def axis2(p, d):
        return to_xy(0, d) if p == 0 else to_xy(d, 0)

    def block(p, o, h=None):
        at = qid(*o)
        if h is None:
            return rows.at[at, p]
        return rows.at[at, p, pl.ds(HT * h, HT)]

    sides = ((0, -1, 1), (1, 1, -1))

    def spread(p, d, o, axis):
        send("g", ("ring", p, d, 0), block(p, o), block(p, o), axis(p, 1))
        send("g", ("ring", p, d, 1), block(p, o), block(p, o), axis(p, -1))
        if d not in RING_G[p]:
            send("g", ("ring", p, d, 2), block(p, o), block(p, o), axis(p, 2))

    def forward(p, d, o, s, axis):
        if d in RING_G[p]:
            send("g", ("ring", p, d, 2), block(p, o, s), block(p, o, s), axis(p, sides[s][2]))

    def tree(op, values):
        while len(values) > 1:
            values = [op(*values[i : i + 2]) if i + 1 < len(values) else values[i] for i in range(0, len(values), 2)]
        return values[0]

    def merge(buf, n):
        each = [buf[i, 0:1] for i in range(n)]
        m = tree(jnp.maximum, each)
        return m + jnp.log(tree(jnp.add, [jnp.exp(e - m) for e in each]))

    def total(buf, n):
        return tree(jnp.add, [buf[i, 1:2] for i in range(n)])

    have = {}
    ready = [(0, 0)]

    def arrived(p, o):
        have[o] = have.get(o, 0) + 1
        if have[o] == 2:
            ready.append(o)

    def start(p):
        got("z%d" % p, zrow.at[p, pl.ds(0, NZ - 1)])
        mine = dot(hot_all[...], zrow[p].reshape(NZ * SLOTS, HF), ((1,), (0,)))
        rows[q_me, p] = mine.astype(BF16)
        spread(p, "one", (0, 0), axis1)
        spread(p, 0, (0, 0), axis2)

    def first(p):
        for s, frm, to in sides:
            o = off(p, frm, 0)
            got(("ring", p, "one", s), block(p, o))
            forward(p, "one", o, s, axis1)
            spread(p, frm, o, axis2)
            arrived(p, o)
        for s, frm, to in sides:
            o = off(p, 0, frm)
            got(("ring", p, 0, s), block(p, o))
            forward(p, 0, o, s, axis2)
            arrived(p, o)
        o = off(p, 2, 0)
        got(("ring", p, "one", 2), block(p, o))
        spread(p, 2, o, axis2)
        arrived(p, o)

    start(0)
    got("xt", xt.at[pl.ds(0, NX * NY - 1)])
    zt[me, 0:1] = merge(xt, NX * NY)
    zt[me, 1:2] = total(xt, NX * NY)
    for o in pairs:
        send("zt", "zt", zt.at[me], zt.at[me], to_pair(*o))
    start(1)
    first(0)
    first(1)
    stu[...] = jnp.zeros_like(stu)
    for cp in loads:
        cp.wait()
    got("zt", zt.at[pl.ds(0, NP - 1)])
    lse_t = merge(zt, NP)
    spots = jnp.zeros((TOK, SLOTS), F32)

    def inverse(s):
        return lax.rsqrt((zt[NC * s, 1:2, 0:SLOTS] + zt[NC * s + 1, 1:2, 0:SLOTS]) / (NV * FC) + EPS)

    for s in range(NZ):
        spots = spots + hot[s].astype(F32) * inverse(s)
    inv_wide = jnp.broadcast_to(jnp.sum(spots, axis=1, keepdims=True), (TOK, FC))

    def drain():
        while ready:
            q = qid(*ready.pop(0))
            raw = jnp.concatenate([rows[q, 0], rows[q, 1]], axis=1)
            normed = (raw.astype(F32) * inv_wide * gain(NC * q + c)).astype(BF16)
            stu[...] += dot(normed, head[q], ((1,), (0,)))

    got("hd", head_side)
    drain()
    for d in (1, -1):
        for p in (0, 1):
            for s, frm, to in sides:
                o = off(p, d, frm)
                got(("ring", p, d, s), block(p, o))
                forward(p, d, o, s, axis2)
                arrived(p, o)
        drain()
    got("tc", teacher_sib)
    tea = jnp.concatenate([tea, teacher_sib[...].astype(F32).T], axis=0)
    prob = jnp.exp(tea - lse_t)
    weight = (layer_ref[...].astype(F32) + 1.0) / LAYERS
    for d in (0, 2, 1, -1):
        for p in (0, 1):
            if d == 2:
                for s, frm, to in sides:
                    o = off(p, d, frm)
                    got(("ring", p, d, s), block(p, o))
                    forward(p, d, o, s, axis2)
                    arrived(p, o)
            o = off(p, d, 2)
            got(("ring", p, d, 2), block(p, o))
            arrived(p, o)
        drain()
    send("st", "st", stu, stu_in, sibling)
    got("st", stu_in)
    student = jnp.concatenate([(stu[:, :FC] + stu_in[:, FC:]).T, (stu[:, FC:] + stu_in[:, :FC]).T], axis=0)
    m = jnp.max(student, axis=0, keepdims=True)
    zs[z, 0:1] = m + jnp.log(jnp.sum(jnp.exp(student - m), axis=0, keepdims=True))
    zs[z, 1:2] = jnp.sum(prob * (tea - student), axis=0, keepdims=True)
    for d in PEERS_Z:
        send("zs", "zs", zs.at[z], zs.at[z], to_z(d))
    got("zs", zs.at[pl.ds(0, NZ - 1)])
    xs[q_me, 0:1] = merge(zs, NZ)
    xs[q_me, 1:2] = total(zs, NZ)
    for o in PEERS_XY:
        send("xs", "xs", xs.at[q_me], xs.at[q_me], to_xy(*o))
    got("xs", xs.at[pl.ds(0, NX * NY - 1)])
    lse_s = merge(xs, NX * NY)
    kl = total(xs, NX * NY) - lse_t + lse_s
    dlogit = (weight * (jnp.exp(student - lse_s) - prob)).T.astype(BF16)
    def own(o):
        return PLANE.index(o)

    def slot(d):
        return OFFS.index(d) if d != "one" else 4

    def chunk_at(p, d, d1):
        return own(off(p, d1, 0)) if d == "one" else own(off(p, d, d1))

    def give(p, d, d1, axis, value):
        i, k = chunk_at(p, d, d1), slot(d)
        if d1 != 0 and d not in RING_R[p]:
            j = (1, -1, 2).index(d1)
            full_out[p, k, j] = value.astype(BF16)
            send("r", ("ring", p, d, 2), full_out.at[p, k, j], full_in.at[p, k, j], axis(p, d1))
        elif d1 == 2:
            for h in (0, 1):
                half_out[p, k, h] = value[HT * h : HT * (h + 1)].astype(BF16)
                send("r", ("ring", p, d, h), half_out.at[p, k, h], half_in.at[p, k, h], axis(p, 1 - 2 * h))
        else:
            part_sum[i, p] = value

    def pass_on(p, d, axis):
        if d not in RING_R[p]:
            return
        k = slot(d)
        for s in (0, 1):
            i = chunk_at(p, d, 1 - 2 * s)
            got(("ring", p, d, s), half_in.at[p, k, s])
            near = pl.ds(HT * s, HT)
            rest = pl.ds(HT * (1 - s), HT)
            full_out[p, k, s, near] = (part_sum[i, p, near] + half_in[p, k, s].astype(F32)).astype(BF16)
            full_out[p, k, s, rest] = part_sum[i, p, rest].astype(BF16)
            send("r", ("ring", p, d, 2), full_out.at[p, k, s], full_in.at[p, k, s], axis(p, 1 - 2 * s))

    def collect(p, d):
        i, k = chunk_at(p, d, 0), slot(d)
        n = 2 if d in RING_R[p] else 3
        got(("ring", p, d, 2), full_in.at[p, k, pl.ds(0, n)])
        value = part_sum[i, p]
        for j in range(n):
            value = value + full_in[p, k, j].astype(F32)
        return value

    for o in FAR:
        value = dot(dlogit, head[qid(*o)], ((1,), (1,)))
        for p in (0, 1):
            d1, d2 = o[::-1] if p == 0 else o
            give(p, d2, d1, axis2, value[:, HF * p : HF * (p + 1)])

    for d in (2, 1, -1):
        for p in (0, 1):
            pass_on(p, d, axis2)
        for p in (0, 1):
            if d == 2:
                give(p, "one", d, axis1, collect(p, d))
    for p in (0, 1):
        pass_on(p, 0, axis2)
    for d in (1, -1):
        for p in (0, 1):
            give(p, "one", d, axis1, collect(p, d))
    for p in (0, 1):
        pass_on(p, "one", axis1)
    for p in (0, 1):
        part_sum[own((0, 0)), p] = collect(p, 0)

    hot_own = hot[z]
    pick4 = lax.broadcasted_iota(jnp.int32, (16, SLOTS), 0)
    pick4 = jnp.where(pick4 < 2, 2 * v + pick4, 2 * vid(0, 0, other) + pick4 - 2)
    pick4 = (pick4 == lax.broadcasted_iota(jnp.int32, (16, SLOTS), 1)).astype(F32)
    sel = dot(pick4.astype(BF16), hot_own, ((1,), (1,))).astype(BF16)
    own_inv = inverse(z) * jnp.where(slot_iota < count_ref[z], 1.0, 0.0)
    inv_four = jnp.sum(pick4[0:4] * own_inv, axis=1, keepdims=True)
    inv_two = inv_four[0:2]
    for q in range(NX * NY):
        for p in (0, 1):
            four = dot(sel, rows[q, p], ((1,), (0,)))[0:4] * inv_four
            at = slice(FC * q + HF * p, FC * q + HF * (p + 1))
            unit_own[:, at] = four[0:2]
            unit_out[:, at] = four[2:4]
    send("un", "un", unit_out, unit_sib, sibling)
    kl_col = jnp.broadcast_to(kl, (HF, TOK)).T
    out_ref[0:1, NV * FC : NV * FC + SLOTS] = jnp.sum(hot_own.astype(F32) * kl_col[:, :SLOTS], axis=0, keepdims=True)
    out_ref[1:2, NV * FC : NV * FC + 1] = jnp.sum(weight * kl, axis=1, keepdims=True) / TOK

    for p in (0, 1):
        whole = collect(p, "one").astype(BF16)
        spread_rows = dot(hot_t[...].reshape(NZ * SLOTS, TOK), whole, ((1,), (0,))).astype(BF16)
        for s in range(NZ):
            for k in range(NC):
                at = SLOTS * s + 32 * k
                z_out[p, NC * s + k] = spread_rows[at : at + 32]
        for d, k in pairs:
            to = NC * zid(d) + (c if k == 0 else other)
            send("zg%d" % p, "zg%d" % p, z_out.at[p, to], z_in.at[p, me], to_pair(d, k))
        z_in[p, me] = z_out[p, me]
    grads = []
    for p in (0, 1):
        got("zg%d" % p, z_in.at[p, pl.ds(0, NP - 1)])
        for k in range(NC):
            value = z_in[p, k].astype(F32)
            for s in range(1, NZ):
                value = value + z_in[p, NC * s + k].astype(F32)
            grads.append(value)
    grads = jnp.concatenate([grads[0], grads[2], grads[1], grads[3]], axis=1)
    for q in range(NX * NY):
        tr_out[q] = grads[2 * q : 2 * q + 2]
    for o in PEERS_XY:
        send("tr", "tr", tr_out.at[qid(*o)], tr_in.at[q_me], to_xy(*o))
    tr_in[q_me] = tr_out[q_me]
    got("tr", tr_in.at[pl.ds(0, NX * NY - 1)])
    got("un", unit_sib)
    both = []
    units = []
    acc = jnp.zeros((2, FC), F32)
    for i in range(NV):
        at = slice(FC * (i // 2), FC * (i // 2 + 1))
        units.append(jnp.where(c == i % 2, unit_own[:, at], unit_sib[:, at]))
        both.append(tr_in[i // 2, :, FC * (i % 2) : FC * (i % 2 + 1)] * gain(i))
        acc = acc + both[i] * units[i]
    mean = jnp.sum(acc, axis=1, keepdims=True) / (NV * FC)
    for i in range(NV):
        out_ref[:, FC * i : FC * (i + 1)] = inv_two * (both[i] - units[i] * mean)
    for k in ("z0", "z1"):
        sent(k, zrow.at[0, pl.ds(0, NZ - 1)])
    sent("zt", zt.at[pl.ds(0, NP - 1)])
    sent("zs", zt.at[pl.ds(0, NZ - 1)])
    for k in ("xt", "xs"):
        sent(k, xt.at[pl.ds(0, NX * NY - 1)])
    for k in ("g", "r"):
        sent(k, rows.at[pl.ds(0, 15)])
    sent("hd", head_side)
    sent("st", stu_in)
    sent("tc", teacher_sib)
    sent("un", unit_out)
    for k in ("zg0", "zg1"):
        sent(k, z_out.at[0, pl.ds(0, NP - 1)])
    sent("tr", tr_out.at[pl.ds(0, NX * NY - 1)])


def on_device(section_hidden, norm_gain, head, teacher_logits, exit_layer, row_count, row_index):
    packed = pl.pallas_call(
        kernel,
        out_shape=pltpu.VMEM((2, NV * FC + 128), F32),
        in_specs=[pl.BlockSpec(memory_space=pltpu.HBM)] * 7,
        out_specs=pl.BlockSpec(memory_space=pltpu.VMEM),
        scratch_shapes=[
            pltpu.VMEM((1, TOK, FC), BF16),
            pltpu.VMEM((2 * NV, 128), F32),
            pltpu.VMEM((TOK, FC), BF16),
            pltpu.VMEM((1, TOK), jnp.int32),
            pltpu.SMEM((NZ,), jnp.int32),
            pltpu.VMEM((NZ, SLOTS), jnp.int32),
            pltpu.VMEM((NX * NY, FC, NC * FC), BF16),
            pltpu.VMEM((NX * NY, 2, TOK, HF), BF16),
            pltpu.VMEM((2, NZ, SLOTS, HF), BF16),
            pltpu.VMEM((NP, 2, TOK), F32),
            pltpu.VMEM((NZ, 2, TOK), F32),
            pltpu.VMEM((NX * NY, 2, TOK), F32),
            pltpu.VMEM((NX * NY, 2, TOK), F32),
            pltpu.VMEM((NZ, TOK, SLOTS), BF16),
            pltpu.VMEM((TOK, NZ * SLOTS), BF16),
            pltpu.VMEM((NZ, SLOTS, TOK), BF16),
            pltpu.VMEM((TOK, FC), BF16),
            pltpu.VMEM((NX * NY, 2, TOK, HF), F32),
            pltpu.VMEM((2, 5, 2, HT, HF), BF16),
            pltpu.VMEM((2, 5, 2, HT, HF), BF16),
            pltpu.VMEM((2, 5, 3, TOK, HF), BF16),
            pltpu.VMEM((2, 5, 3, TOK, HF), BF16),
            pltpu.VMEM((2, NP, 32, HF), BF16),
            pltpu.VMEM((2, NP, 32, HF), BF16),
            pltpu.VMEM((NX * NY, 2, NC * FC), F32),
            pltpu.VMEM((NX * NY, 2, NC * FC), F32),
            pltpu.VMEM((2, NX * NY * FC), F32),
            pltpu.VMEM((2, NX * NY * FC), F32),
            pltpu.VMEM((2, NX * NY * FC), F32),
            pltpu.VMEM((TOK, NC * FC), F32),
            pltpu.VMEM((TOK, NC * FC), F32),
            pltpu.SemaphoreType.DMA((6,)),
            pltpu.SemaphoreType.DMA((4,)),
            pltpu.SemaphoreType.DMA((len(GROUPS),)),
            pltpu.SemaphoreType.DMA((len(NAMES),)),
        ],
        compiler_params=pltpu.CompilerParams(collective_id=0, has_side_effects=True, vmem_limit_bytes=60 * 2**20),
        name="exit_loss",
    )(
        section_hidden,
        norm_gain.reshape(2 * NV, 128),
        head.reshape(NX * NY, NC, FC, head.shape[1]),
        teacher_logits,
        exit_layer.reshape(1, TOK),
        row_count,
        row_index,
    )
    wide = NV * FC
    return packed[0:1, wide : wide + SLOTS], packed[1, wide], packed[None, :, :wide].astype(BF16)


def solution(mesh):
    return jax.shard_map(
        on_device,
        mesh=mesh,
        in_specs=(
            P("section", None, "vocab"),
            P(),
            P(None, ("section", "vocab")),
            P(None, ("section", "vocab")),
            P(),
            P(),
            P(),
        ),
        out_specs=(P("section", None), P(), P("section", "vocab", None)),
        check_vma=False,
    )
```

```python
import jax
import jax.numpy as jnp
from jax import lax
from jax.experimental import pallas as pl
from jax.experimental.pallas import tpu as pltpu
from jax.sharding import PartitionSpec as P

LAYERS = 80
EPS = 1e-05
F32 = jnp.float32
BF16 = jnp.bfloat16
MESH = pl.DeviceIdType.MESH

NZ, NX, NY, NC = 8, 4, 4, 2
NV = NX * NY * NC
TOK = 256
SLOTS = 64
FC = 256
HF = FC // 2
HT = TOK // 2
OFFS = (0, 1, -1, 2)
PLANE = [(a, b) for a in OFFS for b in OFFS]
PEERS_XY = sorted((o for o in PLANE if o != (0, 0)), key=lambda o: -abs(o[0]) - abs(o[1]))
PEERS_Z = (4, 3, -3, 2, -2, 1, -1)
NP = NZ * NC
FAR = [(2, 2), (2, 1), (1, 2), (2, -1), (-1, 2), (2, 0), (0, 2), (1, 1), (-1, 1), (1, -1), (-1, -1), (0, 1), (1, 0), (0, -1), (-1, 0), (0, 0)]


RING_G = ((0,), (0,))
RING_R = ((0,), (0,))


def all_names():
    names = ["z0", "z1", "zt", "xt", "zs", "xs", "zg0", "zg1", "tr", "hd", "st", "tc", "un"]
    names += [("ring", p, d, k) for p in (0, 1) for d in OFFS + ("one",) for k in range(3)]
    return {k: i for i, k in enumerate(names)}


NAMES = all_names()
GROUPS = {k: i for i, k in enumerate(["z0", "z1", "zt", "xt", "zs", "xs", "zg0", "zg1", "tr", "g", "r", "hd", "st", "tc", "un"])}


def dot(a, b, dims):
    return lax.dot_general(a, b, (dims, ((), ())), preferred_element_type=F32)


def kernel(
    hidden_hbm, gain_hbm, head_hbm, teacher_hbm, layer_hbm, count_hbm, index_hbm,
    out_ref,
    hidden_ref, gain_ref, teacher_ref, layer_ref, count_ref, index_ref, head,
    rows, zrow, zt, zs, xt, xs,
    hot, hot_all, hot_t, teacher_sib, part_sum, half_out, half_in, full_out, full_in,
    z_out, z_in, tr_out, tr_in, unit_own, unit_out, unit_sib,
    stu, stu_in, load_sem, head_sem, send_sem, recv_sem,
):
    z = lax.axis_index("section")
    v = lax.axis_index("vocab")
    x, y, c = v // (NY * NC), lax.rem(v // NC, NY), lax.rem(v, NC)
    other = 1 - c

    def qid(dx, dy):
        return lax.rem(x + dx + NX, NX) * NY + lax.rem(y + dy + NY, NY)

    def vid(dx, dy, core):
        return qid(dx, dy) * NC + core

    def zid(dz):
        return lax.rem(z + dz + NZ, NZ)

    def to_xy(dx, dy):
        return (z, vid(dx, dy, c))

    def to_z(dz):
        return (zid(dz), v)

    def column(dz, core):
        return (zid(dz), vid(0, 0, core))

    sibling = (z, vid(0, 0, other))
    pairs = [(d, k) for d in PEERS_Z for k in (0, 1)] + [(0, 1)]
    me = z * NC + c

    def to_pair(d, k):
        return column(d, c if k == 0 else other)

    def send(group, name, src, dst, target):
        pltpu.make_async_remote_copy(
            src_ref=src, dst_ref=dst, send_sem=send_sem.at[GROUPS[group]], recv_sem=recv_sem.at[NAMES[name]],
            device_id=target, device_id_type=MESH).start()

    def got(name, dst):
        pltpu.make_async_copy(dst, dst, recv_sem.at[NAMES[name]]).wait()

    def sent(group, src):
        pltpu.make_async_copy(src, src, send_sem.at[GROUPS[group]]).wait()

    def gain(chunk):
        return jnp.concatenate([gain_ref[pl.ds(2 * chunk, 1), :], gain_ref[pl.ds(2 * chunk + 1, 1), :]], axis=1)

    barrier = pltpu.get_barrier_semaphore()
    partners = [to_pair(*o) for o in pairs] + [to_xy(*o) for o in PEERS_XY]
    for t in partners:
        pl.semaphore_signal(barrier, inc=1, device_id=t, device_id_type=MESH)
    small = [(index_hbm, index_ref), (hidden_hbm, hidden_ref), (teacher_hbm, teacher_ref), (count_hbm, count_ref), (gain_hbm, gain_ref), (layer_hbm, layer_ref)]
    small = [pltpu.make_async_copy(a, b, load_sem.at[i]) for i, (a, b) in enumerate(small)]
    loads = [pltpu.make_async_copy(head_hbm.at[pl.ds(4 * i, 4), c], head.at[pl.ds(4 * i, 4), :, pl.ds(0, FC)], head_sem.at[i]) for i in range(4)]
    for cp in small + loads:
        cp.start()
    for cp in small:
        cp.wait()

    tok_iota = lax.broadcasted_iota(jnp.int32, (TOK, SLOTS), 0)
    slot_iota = lax.broadcasted_iota(jnp.int32, (1, SLOTS), 1)
    own_row = index_ref[pl.ds(z, 1), :]
    pick = (tok_iota == own_row).astype(F32).astype(BF16)
    picked = dot(pick, hidden_ref[0], ((0,), (0,))).astype(BF16)
    for p in (0, 1):
        zrow[p, z] = picked[:, HF * p : HF * (p + 1)]
    squares = picked.astype(F32)
    squares = squares * squares
    squares = (squares[:, :HF] + squares[:, HF:]).T
    q_me = qid(0, 0)
    tea = teacher_ref[...].astype(F32).T
    top = jnp.max(tea, axis=0, keepdims=True)
    xt[q_me, 0:1] = top + jnp.log(jnp.sum(jnp.exp(tea - top), axis=0, keepdims=True))
    xt[q_me, 1:2, 0:SLOTS] = jnp.sum(squares, axis=0, keepdims=True)
    for s in range(NZ):
        live_row = jnp.where(slot_iota < count_ref[s], index_ref[s : s + 1, :], -1)
        hot[s] = (tok_iota == live_row).astype(F32).astype(BF16)
        hot_all[:, SLOTS * s : SLOTS * (s + 1)] = hot[s]
    pl.semaphore_wait(barrier, len(partners))
    for d in PEERS_Z:
        send("z0", "z0", zrow.at[0, z], zrow.at[0, z], to_z(d))
    for o in PEERS_XY:
        send("xt", "xt", xt.at[q_me], xt.at[q_me], to_xy(*o))
    for d in PEERS_Z:
        send("z1", "z1", zrow.at[1, z], zrow.at[1, z], to_z(d))

    head_side = head.at[:, :, pl.ds(FC, FC)]
    send("tc", "tc", teacher_ref, teacher_sib, sibling)

    row = lax.broadcasted_iota(jnp.int32, (SLOTS, SLOTS), 0)
    col = lax.broadcasted_iota(jnp.int32, (SLOTS, SLOTS), 1)
    perm = (row == 4 * ((col % 32) // 2) + 2 * (col // 32) + col % 2).astype(F32).astype(BF16)
    for s in range(NZ):
        hot_t[s] = dot(hot[s], perm, ((1,), (0,))).T.astype(BF16)

    def off(p, d1, d2):
        return (d1, d2) if p == 0 else (d2, d1)

    def axis1(p, d):
        return to_xy(d, 0) if p == 0 else to_xy(0, d)

    def axis2(p, d):
        return to_xy(0, d) if p == 0 else to_xy(d, 0)

    def block(p, o, h=None):
        at = qid(*o)
        if h is None:
            return rows.at[at, p]
        return rows.at[at, p, pl.ds(HT * h, HT)]

    sides = ((0, -1, 1), (1, 1, -1))

    def spread(p, d, o, axis):
        send("g", ("ring", p, d, 0), block(p, o), block(p, o), axis(p, 1))
        send("g", ("ring", p, d, 1), block(p, o), block(p, o), axis(p, -1))
        if d not in RING_G[p]:
            send("g", ("ring", p, d, 2), block(p, o), block(p, o), axis(p, 2))

    def forward(p, d, o, s, axis):
        if d in RING_G[p]:
            send("g", ("ring", p, d, 2), block(p, o, s), block(p, o, s), axis(p, sides[s][2]))

    def tree(op, values):
        while len(values) > 1:
            values = [op(*values[i : i + 2]) if i + 1 < len(values) else values[i] for i in range(0, len(values), 2)]
        return values[0]

    def merge(buf, n):
        each = [buf[i, 0:1] for i in range(n)]
        m = tree(jnp.maximum, each)
        return m + jnp.log(tree(jnp.add, [jnp.exp(e - m) for e in each]))

    def total(buf, n):
        return tree(jnp.add, [buf[i, 1:2] for i in range(n)])

    have = {}
    ready = [(0, 0)]

    def arrived(p, o):
        have[o] = have.get(o, 0) + 1
        if have[o] == 2:
            ready.append(o)

    def start(p):
        got("z%d" % p, zrow.at[p, pl.ds(0, NZ - 1)])
        mine = dot(hot_all[...], zrow[p].reshape(NZ * SLOTS, HF), ((1,), (0,)))
        rows[q_me, p] = mine.astype(BF16)
        spread(p, "one", (0, 0), axis1)
        spread(p, 0, (0, 0), axis2)

    def first(p):
        for s, frm, to in sides:
            o = off(p, frm, 0)
            got(("ring", p, "one", s), block(p, o))
            forward(p, "one", o, s, axis1)
            spread(p, frm, o, axis2)
            arrived(p, o)
        for s, frm, to in sides:
            o = off(p, 0, frm)
            got(("ring", p, 0, s), block(p, o))
            forward(p, 0, o, s, axis2)
            arrived(p, o)
        o = off(p, 2, 0)
        got(("ring", p, "one", 2), block(p, o))
        spread(p, 2, o, axis2)
        arrived(p, o)

    start(0)
    got("xt", xt.at[pl.ds(0, NX * NY - 1)])
    zt[me, 0:1] = merge(xt, NX * NY)
    zt[me, 1:2] = total(xt, NX * NY)
    for o in pairs:
        send("zt", "zt", zt.at[me], zt.at[me], to_pair(*o))
    start(1)
    send("hd", "hd", head_hbm.at[:, other], head_side, sibling)
    first(0)
    first(1)
    stu[...] = jnp.zeros_like(stu)
    for cp in loads:
        cp.wait()
    got("zt", zt.at[pl.ds(0, NP - 1)])
    lse_t = merge(zt, NP)
    spots = jnp.zeros((TOK, SLOTS), F32)

    def inverse(s):
        return lax.rsqrt((zt[NC * s, 1:2, 0:SLOTS] + zt[NC * s + 1, 1:2, 0:SLOTS]) / (NV * FC) + EPS)

    for s in range(NZ):
        spots = spots + hot[s].astype(F32) * inverse(s)
    inv_wide = jnp.broadcast_to(jnp.sum(spots, axis=1, keepdims=True), (TOK, FC))

    def drain():
        while ready:
            q = qid(*ready.pop(0))
            raw = jnp.concatenate([rows[q, 0], rows[q, 1]], axis=1)
            normed = (raw.astype(F32) * inv_wide * gain(NC * q + c)).astype(BF16)
            stu[...] += dot(normed, head[q], ((1,), (0,)))

    got("hd", head_side)
    drain()
    for d in (1, -1):
        for p in (0, 1):
            for s, frm, to in sides:
                o = off(p, d, frm)
                got(("ring", p, d, s), block(p, o))
                forward(p, d, o, s, axis2)
                arrived(p, o)
        drain()
    got("tc", teacher_sib)
    tea = jnp.concatenate([tea, teacher_sib[...].astype(F32).T], axis=0)
    prob = jnp.exp(tea - lse_t)
    weight = (layer_ref[...].astype(F32) + 1.0) / LAYERS
    for d in (0, 2, 1, -1):
        for p in (0, 1):
            if d == 2:
                for s, frm, to in sides:
                    o = off(p, d, frm)
                    got(("ring", p, d, s), block(p, o))
                    forward(p, d, o, s, axis2)
                    arrived(p, o)
            o = off(p, d, 2)
            got(("ring", p, d, 2), block(p, o))
            arrived(p, o)
        drain()
    send("st", "st", stu, stu_in, sibling)
    got("st", stu_in)
    student = jnp.concatenate([(stu[:, :FC] + stu_in[:, FC:]).T, (stu[:, FC:] + stu_in[:, :FC]).T], axis=0)
    m = jnp.max(student, axis=0, keepdims=True)
    zs[z, 0:1] = m + jnp.log(jnp.sum(jnp.exp(student - m), axis=0, keepdims=True))
    zs[z, 1:2] = jnp.sum(prob * (tea - student), axis=0, keepdims=True)
    for d in PEERS_Z:
        send("zs", "zs", zs.at[z], zs.at[z], to_z(d))
    got("zs", zs.at[pl.ds(0, NZ - 1)])
    xs[q_me, 0:1] = merge(zs, NZ)
    xs[q_me, 1:2] = total(zs, NZ)
    for o in PEERS_XY:
        send("xs", "xs", xs.at[q_me], xs.at[q_me], to_xy(*o))
    got("xs", xs.at[pl.ds(0, NX * NY - 1)])
    lse_s = merge(xs, NX * NY)
    kl = total(xs, NX * NY) - lse_t + lse_s
    dlogit = (weight * (jnp.exp(student - lse_s) - prob)).T.astype(BF16)
    def own(o):
        return PLANE.index(o)

    def slot(d):
        return OFFS.index(d) if d != "one" else 4

    def chunk_at(p, d, d1):
        return own(off(p, d1, 0)) if d == "one" else own(off(p, d, d1))

    def give(p, d, d1, axis, value):
        i, k = chunk_at(p, d, d1), slot(d)
        if d1 != 0 and d not in RING_R[p]:
            j = (1, -1, 2).index(d1)
            full_out[p, k, j] = value.astype(BF16)
            send("r", ("ring", p, d, 2), full_out.at[p, k, j], full_in.at[p, k, j], axis(p, d1))
        elif d1 == 2:
            for h in (0, 1):
                half_out[p, k, h] = value[HT * h : HT * (h + 1)].astype(BF16)
                send("r", ("ring", p, d, h), half_out.at[p, k, h], half_in.at[p, k, h], axis(p, 1 - 2 * h))
        else:
            part_sum[i, p] = value

    def pass_on(p, d, axis):
        if d not in RING_R[p]:
            return
        k = slot(d)
        for s in (0, 1):
            i = chunk_at(p, d, 1 - 2 * s)
            got(("ring", p, d, s), half_in.at[p, k, s])
            near = pl.ds(HT * s, HT)
            rest = pl.ds(HT * (1 - s), HT)
            full_out[p, k, s, near] = (part_sum[i, p, near] + half_in[p, k, s].astype(F32)).astype(BF16)
            full_out[p, k, s, rest] = part_sum[i, p, rest].astype(BF16)
            send("r", ("ring", p, d, 2), full_out.at[p, k, s], full_in.at[p, k, s], axis(p, 1 - 2 * s))

    def collect(p, d):
        i, k = chunk_at(p, d, 0), slot(d)
        n = 2 if d in RING_R[p] else 3
        got(("ring", p, d, 2), full_in.at[p, k, pl.ds(0, n)])
        value = part_sum[i, p]
        for j in range(n):
            value = value + full_in[p, k, j].astype(F32)
        return value

    for o in FAR:
        value = dot(dlogit, head[qid(*o)], ((1,), (1,)))
        for p in (0, 1):
            d1, d2 = o[::-1] if p == 0 else o
            give(p, d2, d1, axis2, value[:, HF * p : HF * (p + 1)])

    for d in (2, 1, -1):
        for p in (0, 1):
            pass_on(p, d, axis2)
        for p in (0, 1):
            if d == 2:
                give(p, "one", d, axis1, collect(p, d))
    for p in (0, 1):
        pass_on(p, 0, axis2)
    for d in (1, -1):
        for p in (0, 1):
            give(p, "one", d, axis1, collect(p, d))
    for p in (0, 1):
        pass_on(p, "one", axis1)
    for p in (0, 1):
        part_sum[own((0, 0)), p] = collect(p, 0)

    hot_own = hot[z]
    pick4 = lax.broadcasted_iota(jnp.int32, (16, SLOTS), 0)
    pick4 = jnp.where(pick4 < 2, 2 * v + pick4, 2 * vid(0, 0, other) + pick4 - 2)
    pick4 = (pick4 == lax.broadcasted_iota(jnp.int32, (16, SLOTS), 1)).astype(F32)
    sel = dot(pick4.astype(BF16), hot_own, ((1,), (1,))).astype(BF16)
    own_inv = inverse(z) * jnp.where(slot_iota < count_ref[z], 1.0, 0.0)
    inv_four = jnp.sum(pick4[0:4] * own_inv, axis=1, keepdims=True)
    inv_two = inv_four[0:2]
    for q in range(NX * NY):
        for p in (0, 1):
            four = dot(sel, rows[q, p], ((1,), (0,)))[0:4] * inv_four
            at = slice(FC * q + HF * p, FC * q + HF * (p + 1))
            unit_own[:, at] = four[0:2]
            unit_out[:, at] = four[2:4]
    send("un", "un", unit_out, unit_sib, sibling)
    kl_col = jnp.broadcast_to(kl, (HF, TOK)).T
    out_ref[0:1, NV * FC : NV * FC + SLOTS] = jnp.sum(hot_own.astype(F32) * kl_col[:, :SLOTS], axis=0, keepdims=True)
    out_ref[1:2, NV * FC : NV * FC + 1] = jnp.sum(weight * kl, axis=1, keepdims=True) / TOK

    for p in (0, 1):
        whole = collect(p, "one").astype(BF16)
        spread_rows = dot(hot_t[...].reshape(NZ * SLOTS, TOK), whole, ((1,), (0,))).astype(BF16)
        for s in range(NZ):
            for k in range(NC):
                at = SLOTS * s + 32 * k
                z_out[p, NC * s + k] = spread_rows[at : at + 32]
        for d, k in pairs:
            to = NC * zid(d) + (c if k == 0 else other)
            send("zg%d" % p, "zg%d" % p, z_out.at[p, to], z_in.at[p, me], to_pair(d, k))
        z_in[p, me] = z_out[p, me]
    grads = []
    for p in (0, 1):
        got("zg%d" % p, z_in.at[p, pl.ds(0, NP - 1)])
        for k in range(NC):
            value = z_in[p, k].astype(F32)
            for s in range(1, NZ):
                value = value + z_in[p, NC * s + k].astype(F32)
            grads.append(value)
    grads = jnp.concatenate([grads[0], grads[2], grads[1], grads[3]], axis=1)
    for q in range(NX * NY):
        tr_out[q] = grads[2 * q : 2 * q + 2]
    for o in PEERS_XY:
        send("tr", "tr", tr_out.at[qid(*o)], tr_in.at[q_me], to_xy(*o))
    tr_in[q_me] = tr_out[q_me]
    got("tr", tr_in.at[pl.ds(0, NX * NY - 1)])
    got("un", unit_sib)
    both = []
    units = []
    acc = jnp.zeros((2, FC), F32)
    for i in range(NV):
        at = slice(FC * (i // 2), FC * (i // 2 + 1))
        units.append(jnp.where(c == i % 2, unit_own[:, at], unit_sib[:, at]))
        both.append(tr_in[i // 2, :, FC * (i % 2) : FC * (i % 2 + 1)] * gain(i))
        acc = acc + both[i] * units[i]
    mean = jnp.sum(acc, axis=1, keepdims=True) / (NV * FC)
    for i in range(NV):
        out_ref[:, FC * i : FC * (i + 1)] = inv_two * (both[i] - units[i] * mean)
    for k in ("z0", "z1"):
        sent(k, zrow.at[0, pl.ds(0, NZ - 1)])
    sent("zt", zt.at[pl.ds(0, NP - 1)])
    sent("zs", zt.at[pl.ds(0, NZ - 1)])
    for k in ("xt", "xs"):
        sent(k, xt.at[pl.ds(0, NX * NY - 1)])
    for k in ("g", "r"):
        sent(k, rows.at[pl.ds(0, 15)])
    sent("hd", head_side)
    sent("st", stu_in)
    sent("tc", teacher_sib)
    sent("un", unit_out)
    for k in ("zg0", "zg1"):
        sent(k, z_out.at[0, pl.ds(0, NP - 1)])
    sent("tr", tr_out.at[pl.ds(0, NX * NY - 1)])


def on_device(section_hidden, norm_gain, head, teacher_logits, exit_layer, row_count, row_index):
    packed = pl.pallas_call(
        kernel,
        out_shape=pltpu.VMEM((2, NV * FC + 128), F32),
        in_specs=[pl.BlockSpec(memory_space=pltpu.HBM)] * 7,
        out_specs=pl.BlockSpec(memory_space=pltpu.VMEM),
        scratch_shapes=[
            pltpu.VMEM((1, TOK, FC), BF16),
            pltpu.VMEM((2 * NV, 128), F32),
            pltpu.VMEM((TOK, FC), BF16),
            pltpu.VMEM((1, TOK), jnp.int32),
            pltpu.SMEM((NZ,), jnp.int32),
            pltpu.VMEM((NZ, SLOTS), jnp.int32),
            pltpu.VMEM((NX * NY, FC, NC * FC), BF16),
            pltpu.VMEM((NX * NY, 2, TOK, HF), BF16),
            pltpu.VMEM((2, NZ, SLOTS, HF), BF16),
            pltpu.VMEM((NP, 2, TOK), F32),
            pltpu.VMEM((NZ, 2, TOK), F32),
            pltpu.VMEM((NX * NY, 2, TOK), F32),
            pltpu.VMEM((NX * NY, 2, TOK), F32),
            pltpu.VMEM((NZ, TOK, SLOTS), BF16),
            pltpu.VMEM((TOK, NZ * SLOTS), BF16),
            pltpu.VMEM((NZ, SLOTS, TOK), BF16),
            pltpu.VMEM((TOK, FC), BF16),
            pltpu.VMEM((NX * NY, 2, TOK, HF), F32),
            pltpu.VMEM((2, 5, 2, HT, HF), BF16),
            pltpu.VMEM((2, 5, 2, HT, HF), BF16),
            pltpu.VMEM((2, 5, 3, TOK, HF), BF16),
            pltpu.VMEM((2, 5, 3, TOK, HF), BF16),
            pltpu.VMEM((2, NP, 32, HF), BF16),
            pltpu.VMEM((2, NP, 32, HF), BF16),
            pltpu.VMEM((NX * NY, 2, NC * FC), F32),
            pltpu.VMEM((NX * NY, 2, NC * FC), F32),
            pltpu.VMEM((2, NX * NY * FC), F32),
            pltpu.VMEM((2, NX * NY * FC), F32),
            pltpu.VMEM((2, NX * NY * FC), F32),
            pltpu.VMEM((TOK, NC * FC), F32),
            pltpu.VMEM((TOK, NC * FC), F32),
            pltpu.SemaphoreType.DMA((6,)),
            pltpu.SemaphoreType.DMA((4,)),
            pltpu.SemaphoreType.DMA((len(GROUPS),)),
            pltpu.SemaphoreType.DMA((len(NAMES),)),
        ],
        compiler_params=pltpu.CompilerParams(collective_id=0, has_side_effects=True, vmem_limit_bytes=60 * 2**20),
        name="exit_loss",
    )(
        section_hidden,
        norm_gain.reshape(2 * NV, 128),
        head.reshape(NX * NY, NC, FC, head.shape[1]),
        teacher_logits,
        exit_layer.reshape(1, TOK),
        row_count,
        row_index,
    )
    wide = NV * FC
    return packed[0:1, wide : wide + SLOTS], packed[1, wide], packed[None, :, :wide].astype(BF16)


def solution(mesh):
    return jax.shard_map(
        on_device,
        mesh=mesh,
        in_specs=(
            P("section", None, "vocab"),
            P(),
            P(None, ("section", "vocab")),
            P(None, ("section", "vocab")),
            P(),
            P(),
            P(),
        ),
        out_specs=(P("section", None), P(), P("section", "vocab", None)),
        check_vma=False,
    )
```

```python
import jax
import jax.numpy as jnp
from jax import lax
from jax.experimental import pallas as pl
from jax.experimental.pallas import tpu as pltpu
from jax.sharding import PartitionSpec as P

LAYERS = 80
EPS = 1e-05
F32 = jnp.float32
BF16 = jnp.bfloat16
MESH = pl.DeviceIdType.MESH

NZ, NX, NY, NC = 8, 4, 4, 2
NV = NX * NY * NC
TOK = 256
SLOTS = 64
FC = 256
HF = FC // 2
HT = TOK // 2
OFFS = (0, 1, -1, 2)
PLANE = [(a, b) for a in OFFS for b in OFFS]
PEERS_XY = sorted((o for o in PLANE if o != (0, 0)), key=lambda o: -abs(o[0]) - abs(o[1]))
PEERS_Z = (4, 3, -3, 2, -2, 1, -1)
NP = NZ * NC
FAR = [(2, 2), (2, 1), (1, 2), (2, -1), (-1, 2), (2, 0), (0, 2), (1, 1), (-1, 1), (1, -1), (-1, -1), (0, 1), (1, 0), (0, -1), (-1, 0), (0, 0)]


RING_G = ((0,), (0,))
RING_R = ((0,), (0,))


def all_names():
    names = ["z0", "z1", "zt", "xt", "zs", "xs", "zg0", "zg1", "tr", "hd", "st", "tc", "un"]
    names += [("ring", p, d, k) for p in (0, 1) for d in OFFS + ("one",) for k in range(3)]
    return {k: i for i, k in enumerate(names)}


NAMES = all_names()
GROUPS = {k: i for i, k in enumerate(["z0", "z1", "zt", "xt", "zs", "xs", "zg0", "zg1", "tr", "g", "r", "hd", "st", "tc", "un"])}


def dot(a, b, dims):
    return lax.dot_general(a, b, (dims, ((), ())), preferred_element_type=F32)


def kernel(
    hidden_hbm, gain_hbm, head_hbm, teacher_hbm, layer_hbm, count_hbm, index_hbm,
    out_ref,
    hidden_ref, gain_ref, teacher_ref, layer_ref, count_ref, index_ref, head,
    rows, zrow, zt, zs, xt, xs,
    hot, hot_all, hot_t, teacher_sib, part_sum, half_out, half_in, full_out, full_in,
    z_out, z_in, tr_out, tr_in, unit_own, unit_out, unit_sib,
    stu, stu_in, load_sem, head_sem, send_sem, recv_sem,
):
    z = lax.axis_index("section")
    v = lax.axis_index("vocab")
    x, y, c = v // (NY * NC), lax.rem(v // NC, NY), lax.rem(v, NC)
    other = 1 - c

    def qid(dx, dy):
        return lax.rem(x + dx + NX, NX) * NY + lax.rem(y + dy + NY, NY)

    def vid(dx, dy, core):
        return qid(dx, dy) * NC + core

    def zid(dz):
        return lax.rem(z + dz + NZ, NZ)

    def to_xy(dx, dy):
        return (z, vid(dx, dy, c))

    def to_z(dz):
        return (zid(dz), v)

    def column(dz, core):
        return (zid(dz), vid(0, 0, core))

    sibling = (z, vid(0, 0, other))
    pairs = [(d, k) for d in PEERS_Z for k in (0, 1)] + [(0, 1)]
    me = z * NC + c

    def to_pair(d, k):
        return column(d, c if k == 0 else other)

    def send(group, name, src, dst, target):
        pltpu.make_async_remote_copy(
            src_ref=src, dst_ref=dst, send_sem=send_sem.at[GROUPS[group]], recv_sem=recv_sem.at[NAMES[name]],
            device_id=target, device_id_type=MESH).start()

    def got(name, dst):
        pltpu.make_async_copy(dst, dst, recv_sem.at[NAMES[name]]).wait()

    def sent(group, src):
        pltpu.make_async_copy(src, src, send_sem.at[GROUPS[group]]).wait()

    def gain(chunk):
        return jnp.concatenate([gain_ref[pl.ds(2 * chunk, 1), :], gain_ref[pl.ds(2 * chunk + 1, 1), :]], axis=1)

    barrier = pltpu.get_barrier_semaphore()
    partners = [to_pair(*o) for o in pairs] + [to_xy(*o) for o in PEERS_XY]
    for t in partners:
        pl.semaphore_signal(barrier, inc=1, device_id=t, device_id_type=MESH)
    small = [(index_hbm, index_ref), (hidden_hbm, hidden_ref), (teacher_hbm, teacher_ref), (count_hbm, count_ref), (gain_hbm, gain_ref), (layer_hbm, layer_ref)]
    small = [pltpu.make_async_copy(a, b, load_sem.at[i]) for i, (a, b) in enumerate(small)]
    loads = [pltpu.make_async_copy(head_hbm.at[pl.ds(4 * i, 4), c], head.at[pl.ds(4 * i, 4), :, pl.ds(0, FC)], head_sem.at[i]) for i in range(4)]
    for cp in small + loads:
        cp.start()
    for cp in small:
        cp.wait()

    tok_iota = lax.broadcasted_iota(jnp.int32, (TOK, SLOTS), 0)
    slot_iota = lax.broadcasted_iota(jnp.int32, (1, SLOTS), 1)
    own_row = index_ref[pl.ds(z, 1), :]
    pick = (tok_iota == own_row).astype(F32).astype(BF16)
    picked = dot(pick, hidden_ref[0], ((0,), (0,))).astype(BF16)
    for p in (0, 1):
        zrow[p, z] = picked[:, HF * p : HF * (p + 1)]
    squares = picked.astype(F32)
    squares = squares * squares
    squares = (squares[:, :HF] + squares[:, HF:]).T
    q_me = qid(0, 0)
    tea = teacher_ref[...].astype(F32).T
    top = jnp.max(tea, axis=0, keepdims=True)
    xt[q_me, 0:1] = top + jnp.log(jnp.sum(jnp.exp(tea - top), axis=0, keepdims=True))
    xt[q_me, 1:2, 0:SLOTS] = jnp.sum(squares, axis=0, keepdims=True)
    for s in range(NZ):
        live_row = jnp.where(slot_iota < count_ref[s], index_ref[s : s + 1, :], -1)
        hot[s] = (tok_iota == live_row).astype(F32).astype(BF16)
        hot_all[:, SLOTS * s : SLOTS * (s + 1)] = hot[s]
    pl.semaphore_wait(barrier, len(partners))
    for d in PEERS_Z:
        send("z0", "z0", zrow.at[0, z], zrow.at[0, z], to_z(d))
    for o in PEERS_XY:
        send("xt", "xt", xt.at[q_me], xt.at[q_me], to_xy(*o))
    for d in PEERS_Z:
        send("z1", "z1", zrow.at[1, z], zrow.at[1, z], to_z(d))

    head_side = head.at[:, :, pl.ds(FC, FC)]
    send("tc", "tc", teacher_ref, teacher_sib, sibling)

    row = lax.broadcasted_iota(jnp.int32, (SLOTS, SLOTS), 0)
    col = lax.broadcasted_iota(jnp.int32, (SLOTS, SLOTS), 1)
    perm = (row == 4 * ((col % 32) // 2) + 2 * (col // 32) + col % 2).astype(F32).astype(BF16)
    for s in range(NZ):
        hot_t[s] = dot(hot[s], perm, ((1,), (0,))).T.astype(BF16)

    def off(p, d1, d2):
        return (d1, d2) if p == 0 else (d2, d1)

    def axis1(p, d):
        return to_xy(d, 0) if p == 0 else to_xy(0, d)

    def axis2(p, d):
        return to_xy(0, d) if p == 0 else to_xy(d, 0)

    def block(p, o, h=None):
        at = qid(*o)
        if h is None:
            return rows.at[at, p]
        return rows.at[at, p, pl.ds(HT * h, HT)]

    sides = ((0, -1, 1), (1, 1, -1))

    def spread(p, d, o, axis):
        send("g", ("ring", p, d, 0), block(p, o), block(p, o), axis(p, 1))
        send("g", ("ring", p, d, 1), block(p, o), block(p, o), axis(p, -1))
        if d not in RING_G[p]:
            send("g", ("ring", p, d, 2), block(p, o), block(p, o), axis(p, 2))

    def forward(p, d, o, s, axis):
        if d in RING_G[p]:
            send("g", ("ring", p, d, 2), block(p, o, s), block(p, o, s), axis(p, sides[s][2]))

    def tree(op, values):
        while len(values) > 1:
            values = [op(*values[i : i + 2]) if i + 1 < len(values) else values[i] for i in range(0, len(values), 2)]
        return values[0]

    def merge(buf, n):
        each = [buf[i, 0:1] for i in range(n)]
        m = tree(jnp.maximum, each)
        return m + jnp.log(tree(jnp.add, [jnp.exp(e - m) for e in each]))

    def total(buf, n):
        return tree(jnp.add, [buf[i, 1:2] for i in range(n)])

    have = {}
    ready = [(0, 0)]

    def arrived(p, o):
        have[o] = have.get(o, 0) + 1
        if have[o] == 2:
            ready.append(o)

    def start(p):
        got("z%d" % p, zrow.at[p, pl.ds(0, NZ - 1)])
        mine = dot(hot_all[...], zrow[p].reshape(NZ * SLOTS, HF), ((1,), (0,)))
        rows[q_me, p] = mine.astype(BF16)
        spread(p, "one", (0, 0), axis1)
        spread(p, 0, (0, 0), axis2)

    def first(p):
        for s, frm, to in sides:
            o = off(p, frm, 0)
            got(("ring", p, "one", s), block(p, o))
            forward(p, "one", o, s, axis1)
            spread(p, frm, o, axis2)
            arrived(p, o)

    def second(p):
        o = off(p, 2, 0)
        got(("ring", p, "one", 2), block(p, o))
        spread(p, 2, o, axis2)
        arrived(p, o)

    def third(p):
        for s, frm, to in sides:
            o = off(p, 0, frm)
            got(("ring", p, 0, s), block(p, o))
            forward(p, 0, o, s, axis2)
            arrived(p, o)

    start(0)
    got("xt", xt.at[pl.ds(0, NX * NY - 1)])
    zt[me, 0:1] = merge(xt, NX * NY)
    zt[me, 1:2] = total(xt, NX * NY)
    for o in pairs:
        send("zt", "zt", zt.at[me], zt.at[me], to_pair(*o))
    start(1)
    send("hd", "hd", head_hbm.at[:, other], head_side, sibling)
    first(0)
    second(0)
    third(0)
    first(1)
    second(1)
    third(1)
    stu[...] = jnp.zeros_like(stu)
    for cp in loads:
        cp.wait()
    got("zt", zt.at[pl.ds(0, NP - 1)])
    lse_t = merge(zt, NP)
    spots = jnp.zeros((TOK, SLOTS), F32)

    def inverse(s):
        return lax.rsqrt((zt[NC * s, 1:2, 0:SLOTS] + zt[NC * s + 1, 1:2, 0:SLOTS]) / (NV * FC) + EPS)

    for s in range(NZ):
        spots = spots + hot[s].astype(F32) * inverse(s)
    inv_wide = jnp.broadcast_to(jnp.sum(spots, axis=1, keepdims=True), (TOK, FC))

    def drain():
        while ready:
            q = qid(*ready.pop(0))
            raw = jnp.concatenate([rows[q, 0], rows[q, 1]], axis=1)
            normed = (raw.astype(F32) * inv_wide * gain(NC * q + c)).astype(BF16)
            stu[...] += dot(normed, head[q], ((1,), (0,)))

    got("hd", head_side)
    drain()
    for d in (1, -1):
        for p in (0, 1):
            for s, frm, to in sides:
                o = off(p, d, frm)
                got(("ring", p, d, s), block(p, o))
                forward(p, d, o, s, axis2)
                arrived(p, o)
        drain()
    got("tc", teacher_sib)
    tea = jnp.concatenate([tea, teacher_sib[...].astype(F32).T], axis=0)
    prob = jnp.exp(tea - lse_t)
    weight = (layer_ref[...].astype(F32) + 1.0) / LAYERS
    for d in (0, 2, 1, -1):
        for p in (0, 1):
            if d == 2:
                for s, frm, to in sides:
                    o = off(p, d, frm)
                    got(("ring", p, d, s), block(p, o))
                    forward(p, d, o, s, axis2)
                    arrived(p, o)
            o = off(p, d, 2)
            got(("ring", p, d, 2), block(p, o))
            arrived(p, o)
        drain()
    send("st", "st", stu, stu_in, sibling)
    got("st", stu_in)
    student = jnp.concatenate([(stu[:, :FC] + stu_in[:, FC:]).T, (stu[:, FC:] + stu_in[:, :FC]).T], axis=0)
    m = jnp.max(student, axis=0, keepdims=True)
    zs[z, 0:1] = m + jnp.log(jnp.sum(jnp.exp(student - m), axis=0, keepdims=True))
    zs[z, 1:2] = jnp.sum(prob * (tea - student), axis=0, keepdims=True)
    for d in PEERS_Z:
        send("zs", "zs", zs.at[z], zs.at[z], to_z(d))
    got("zs", zs.at[pl.ds(0, NZ - 1)])
    xs[q_me, 0:1] = merge(zs, NZ)
    xs[q_me, 1:2] = total(zs, NZ)
    for o in PEERS_XY:
        send("xs", "xs", xs.at[q_me], xs.at[q_me], to_xy(*o))
    got("xs", xs.at[pl.ds(0, NX * NY - 1)])
    lse_s = merge(xs, NX * NY)
    kl = total(xs, NX * NY) - lse_t + lse_s
    dlogit = (weight * (jnp.exp(student - lse_s) - prob)).T.astype(BF16)
    def own(o):
        return PLANE.index(o)

    def slot(d):
        return OFFS.index(d) if d != "one" else 4

    def chunk_at(p, d, d1):
        return own(off(p, d1, 0)) if d == "one" else own(off(p, d, d1))

    def give(p, d, d1, axis, value):
        i, k = chunk_at(p, d, d1), slot(d)
        if d1 != 0 and d not in RING_R[p]:
            j = (1, -1, 2).index(d1)
            full_out[p, k, j] = value.astype(BF16)
            send("r", ("ring", p, d, 2), full_out.at[p, k, j], full_in.at[p, k, j], axis(p, d1))
        elif d1 == 2:
            for h in (0, 1):
                half_out[p, k, h] = value[HT * h : HT * (h + 1)].astype(BF16)
                send("r", ("ring", p, d, h), half_out.at[p, k, h], half_in.at[p, k, h], axis(p, 1 - 2 * h))
        else:
            part_sum[i, p] = value

    def pass_on(p, d, axis):
        if d not in RING_R[p]:
            return
        k = slot(d)
        for s in (0, 1):
            i = chunk_at(p, d, 1 - 2 * s)
            got(("ring", p, d, s), half_in.at[p, k, s])
            near = pl.ds(HT * s, HT)
            rest = pl.ds(HT * (1 - s), HT)
            full_out[p, k, s, near] = (part_sum[i, p, near] + half_in[p, k, s].astype(F32)).astype(BF16)
            full_out[p, k, s, rest] = part_sum[i, p, rest].astype(BF16)
            send("r", ("ring", p, d, 2), full_out.at[p, k, s], full_in.at[p, k, s], axis(p, 1 - 2 * s))

    def collect(p, d):
        i, k = chunk_at(p, d, 0), slot(d)
        n = 2 if d in RING_R[p] else 3
        got(("ring", p, d, 2), full_in.at[p, k, pl.ds(0, n)])
        value = part_sum[i, p]
        for j in range(n):
            value = value + full_in[p, k, j].astype(F32)
        return value

    for o in FAR:
        value = dot(dlogit, head[qid(*o)], ((1,), (1,)))
        for p in (0, 1):
            d1, d2 = o[::-1] if p == 0 else o
            give(p, d2, d1, axis2, value[:, HF * p : HF * (p + 1)])

    for d in (2, 1, -1):
        for p in (0, 1):
            pass_on(p, d, axis2)
        for p in (0, 1):
            if d == 2:
                give(p, "one", d, axis1, collect(p, d))
    for p in (0, 1):
        pass_on(p, 0, axis2)
    for d in (1, -1):
        for p in (0, 1):
            give(p, "one", d, axis1, collect(p, d))
    for p in (0, 1):
        pass_on(p, "one", axis1)
    for p in (0, 1):
        part_sum[own((0, 0)), p] = collect(p, 0)

    hot_own = hot[z]
    pick4 = lax.broadcasted_iota(jnp.int32, (16, SLOTS), 0)
    pick4 = jnp.where(pick4 < 2, 2 * v + pick4, 2 * vid(0, 0, other) + pick4 - 2)
    pick4 = (pick4 == lax.broadcasted_iota(jnp.int32, (16, SLOTS), 1)).astype(F32)
    sel = dot(pick4.astype(BF16), hot_own, ((1,), (1,))).astype(BF16)
    own_inv = inverse(z) * jnp.where(slot_iota < count_ref[z], 1.0, 0.0)
    inv_four = jnp.sum(pick4[0:4] * own_inv, axis=1, keepdims=True)
    inv_two = inv_four[0:2]
    for q in range(NX * NY):
        for p in (0, 1):
            four = dot(sel, rows[q, p], ((1,), (0,)))[0:4] * inv_four
            at = slice(FC * q + HF * p, FC * q + HF * (p + 1))
            unit_own[:, at] = four[0:2]
            unit_out[:, at] = four[2:4]
    send("un", "un", unit_out, unit_sib, sibling)
    kl_col = jnp.broadcast_to(kl, (HF, TOK)).T
    out_ref[0:1, NV * FC : NV * FC + SLOTS] = jnp.sum(hot_own.astype(F32) * kl_col[:, :SLOTS], axis=0, keepdims=True)
    out_ref[1:2, NV * FC : NV * FC + 1] = jnp.sum(weight * kl, axis=1, keepdims=True) / TOK

    for p in (0, 1):
        whole = collect(p, "one").astype(BF16)
        spread_rows = dot(hot_t[...].reshape(NZ * SLOTS, TOK), whole, ((1,), (0,))).astype(BF16)
        for s in range(NZ):
            for k in range(NC):
                at = SLOTS * s + 32 * k
                z_out[p, NC * s + k] = spread_rows[at : at + 32]
        for d, k in pairs:
            to = NC * zid(d) + (c if k == 0 else other)
            send("zg%d" % p, "zg%d" % p, z_out.at[p, to], z_in.at[p, me], to_pair(d, k))
        z_in[p, me] = z_out[p, me]
    grads = []
    for p in (0, 1):
        got("zg%d" % p, z_in.at[p, pl.ds(0, NP - 1)])
        for k in range(NC):
            value = z_in[p, k].astype(F32)
            for s in range(1, NZ):
                value = value + z_in[p, NC * s + k].astype(F32)
            grads.append(value)
    grads = jnp.concatenate([grads[0], grads[2], grads[1], grads[3]], axis=1)
    for q in range(NX * NY):
        tr_out[q] = grads[2 * q : 2 * q + 2]
    for o in PEERS_XY:
        send("tr", "tr", tr_out.at[qid(*o)], tr_in.at[q_me], to_xy(*o))
    tr_in[q_me] = tr_out[q_me]
    got("tr", tr_in.at[pl.ds(0, NX * NY - 1)])
    got("un", unit_sib)
    both = []
    units = []
    acc = jnp.zeros((2, FC), F32)
    for i in range(NV):
        at = slice(FC * (i // 2), FC * (i // 2 + 1))
        units.append(jnp.where(c == i % 2, unit_own[:, at], unit_sib[:, at]))
        both.append(tr_in[i // 2, :, FC * (i % 2) : FC * (i % 2 + 1)] * gain(i))
        acc = acc + both[i] * units[i]
    mean = jnp.sum(acc, axis=1, keepdims=True) / (NV * FC)
    for i in range(NV):
        out_ref[:, FC * i : FC * (i + 1)] = inv_two * (both[i] - units[i] * mean)
    for k in ("z0", "z1"):
        sent(k, zrow.at[0, pl.ds(0, NZ - 1)])
    sent("zt", zt.at[pl.ds(0, NP - 1)])
    sent("zs", zt.at[pl.ds(0, NZ - 1)])
    for k in ("xt", "xs"):
        sent(k, xt.at[pl.ds(0, NX * NY - 1)])
    for k in ("g", "r"):
        sent(k, rows.at[pl.ds(0, 15)])
    sent("hd", head_side)
    sent("st", stu_in)
    sent("tc", teacher_sib)
    sent("un", unit_out)
    for k in ("zg0", "zg1"):
        sent(k, z_out.at[0, pl.ds(0, NP - 1)])
    sent("tr", tr_out.at[pl.ds(0, NX * NY - 1)])


def on_device(section_hidden, norm_gain, head, teacher_logits, exit_layer, row_count, row_index):
    packed = pl.pallas_call(
        kernel,
        out_shape=pltpu.VMEM((2, NV * FC + 128), F32),
        in_specs=[pl.BlockSpec(memory_space=pltpu.HBM)] * 7,
        out_specs=pl.BlockSpec(memory_space=pltpu.VMEM),
        scratch_shapes=[
            pltpu.VMEM((1, TOK, FC), BF16),
            pltpu.VMEM((2 * NV, 128), F32),
            pltpu.VMEM((TOK, FC), BF16),
            pltpu.VMEM((1, TOK), jnp.int32),
            pltpu.SMEM((NZ,), jnp.int32),
            pltpu.VMEM((NZ, SLOTS), jnp.int32),
            pltpu.VMEM((NX * NY, FC, NC * FC), BF16),
            pltpu.VMEM((NX * NY, 2, TOK, HF), BF16),
            pltpu.VMEM((2, NZ, SLOTS, HF), BF16),
            pltpu.VMEM((NP, 2, TOK), F32),
            pltpu.VMEM((NZ, 2, TOK), F32),
            pltpu.VMEM((NX * NY, 2, TOK), F32),
            pltpu.VMEM((NX * NY, 2, TOK), F32),
            pltpu.VMEM((NZ, TOK, SLOTS), BF16),
            pltpu.VMEM((TOK, NZ * SLOTS), BF16),
            pltpu.VMEM((NZ, SLOTS, TOK), BF16),
            pltpu.VMEM((TOK, FC), BF16),
            pltpu.VMEM((NX * NY, 2, TOK, HF), F32),
            pltpu.VMEM((2, 5, 2, HT, HF), BF16),
            pltpu.VMEM((2, 5, 2, HT, HF), BF16),
            pltpu.VMEM((2, 5, 3, TOK, HF), BF16),
            pltpu.VMEM((2, 5, 3, TOK, HF), BF16),
            pltpu.VMEM((2, NP, 32, HF), BF16),
            pltpu.VMEM((2, NP, 32, HF), BF16),
            pltpu.VMEM((NX * NY, 2, NC * FC), F32),
            pltpu.VMEM((NX * NY, 2, NC * FC), F32),
            pltpu.VMEM((2, NX * NY * FC), F32),
            pltpu.VMEM((2, NX * NY * FC), F32),
            pltpu.VMEM((2, NX * NY * FC), F32),
            pltpu.VMEM((TOK, NC * FC), F32),
            pltpu.VMEM((TOK, NC * FC), F32),
            pltpu.SemaphoreType.DMA((6,)),
            pltpu.SemaphoreType.DMA((4,)),
            pltpu.SemaphoreType.DMA((len(GROUPS),)),
            pltpu.SemaphoreType.DMA((len(NAMES),)),
        ],
        compiler_params=pltpu.CompilerParams(collective_id=0, has_side_effects=True, vmem_limit_bytes=60 * 2**20),
        name="exit_loss",
    )(
        section_hidden,
        norm_gain.reshape(2 * NV, 128),
        head.reshape(NX * NY, NC, FC, head.shape[1]),
        teacher_logits,
        exit_layer.reshape(1, TOK),
        row_count,
        row_index,
    )
    wide = NV * FC
    return packed[0:1, wide : wide + SLOTS], packed[1, wide], packed[None, :, :wide].astype(BF16)


def solution(mesh):
    return jax.shard_map(
        on_device,
        mesh=mesh,
        in_specs=(
            P("section", None, "vocab"),
            P(),
            P(None, ("section", "vocab")),
            P(None, ("section", "vocab")),
            P(),
            P(),
            P(),
        ),
        out_specs=(P("section", None), P(), P("section", "vocab", None)),
        check_vma=False,
    )
```
